32 devices in a mesh: tile: 8 (over y, x, core), col: 4 (over z).
Axes of the slice: x: 2, y: 2, z: 4, core: 2. Of those that a mesh axis runs over, the one named last changes fastest.
Arguments:
- u_velocity: float32 [4096, 2048], P('tile', 'col'), may hold values from -12 to 12
- v_velocity: float32 [4096, 2048], P('tile', 'col'), may hold values from -12 to 12
- ocean_mask: int32 [32, 16], P('tile', 'col'), may hold values from 0 to 1, as said below
- tile_owner: int32 [32, 16], P('tile', 'col'), may hold values from 0 to 7, as said below
- lower_edge_quarter_turns: int32 [8], replicated, may hold values from 0 to 3
Outputs:
- library: float32 [8, 4, 16, 16, 1024], P('tile', 'col')
- gram: float32 [16, 16], replicated
The draws below stay inside these ranges and needn't reach their ends.
Inputs may be any that keep to these rules, and one draw needn't show every extreme that they name: `ocean_mask`: in every column of devices (4 x 4 tile blocks), at least one device has only ocean tiles. `tile_owner`: among the ocean tiles of one device at most 2 share an owner; the ocean tiles of one column of devices are spread over its 8 owners so that the owners' counts differ by at most one. Land tiles carry an owner that is not used.
All inputs are finite; a program needn't handle non-finite values.
Results may differ from the reference program's by a relative error of at most 0.00014.
Values sent between devices are 32-bit elements; how exact they have to be, the bound alone decides.
A program may use at most 192 MiB of HBM per device.

```python
import math
import jax
import jax.numpy as jnp
from jax import lax

CX = 512
CY = 512
PASSES = 8
TS = 32
TERMS = 16
NX = 4096
NY = 2048
GX = 4
GY = 4
TPD = 16
CAP = 2
TC = 1024
N_TILE = 8
N_COL = 4


def rescaled_forcing_field(key):
    key_scale, key_block, key_noise = jax.random.split(key, 3)
    scale = 0.3 * jnp.exp(jax.random.uniform(key_scale, (NX // 32, NY // 32), jnp.float32, 0.0, math.log(10.0)))
    scale = jnp.repeat(jnp.repeat(scale, 32, axis=0), 32, axis=1)
    block = jnp.clip(jax.random.normal(key_block, (NX // 4, NY // 4), jnp.float32), -2.5, 2.5)
    noise = jnp.clip(jax.random.normal(key_noise, (NX, NY), jnp.float32), -2.5, 2.5)
    block = jnp.repeat(jnp.repeat(block, 4, axis=0), 4, axis=1)
    return scale * (block + 0.5 * noise)


def draw_u_velocity(key, part):
    return rescaled_forcing_field(jax.random.fold_in(key, 11))


def draw_v_velocity(key, part):
    return rescaled_forcing_field(jax.random.fold_in(key, 12))


def ocean_tables(key):
    root_random_key = jax.random.fold_in(key, 21)
    level_random_key, key_full, key_roll, key_perm, key_land = jax.random.split(root_random_key, 5)
    level = jax.random.randint(level_random_key, (N_TILE, N_COL), 40, 101)
    full_row = jax.random.randint(key_full, (N_COL,), 0, N_TILE)
    rows_index = jnp.arange(N_TILE, dtype=jnp.int32)
    level = jnp.where(rows_index[:, None] == full_row[None, :], 100, level)
    rolled = jax.random.randint(key_roll, (N_TILE, GX, N_COL, GY), 0, 100)
    mask = (rolled < level[:, None, :, None]).astype(jnp.int32)
    ordered = jnp.transpose(mask, (2, 0, 1, 3)).reshape(N_COL, N_TILE * GX * GY)
    rank = jnp.cumsum(ordered, axis=1) - ordered
    perms = jax.vmap(lambda one: jax.random.permutation(one, N_TILE))(jax.random.split(key_perm, N_COL))
    ocean_owner = jnp.take_along_axis(perms, rank % N_TILE, axis=1)
    land_owner = jax.random.randint(key_land, (N_COL, N_TILE * GX * GY), 0, N_TILE)
    owner = jnp.where(ordered == 1, ocean_owner, land_owner).astype(jnp.int32)
    owner = jnp.transpose(owner.reshape(N_COL, N_TILE, GX, GY), (1, 2, 0, 3)).reshape(N_TILE * GX, N_COL * GY)
    mask = mask.reshape(N_TILE * GX, N_COL * GY)
    return (mask, owner)


def draw_ocean_mask(key, part):
    return ocean_tables(key)[0]


def draw_tile_owner(key, part):
    return ocean_tables(key)[1]


def with_ends(result, own_key, low, top_value):
    longest = result.shape.index(max(result.shape))
    spots = []
    for shift in (0, 1):
        where = [jax.random.randint(jax.random.fold_in(own_key, axis), (), 0, length) for axis, length in enumerate(result.shape)]
        where[longest] = (where[longest] + shift) % result.shape[longest]
        spots.append(tuple(where))
    return result.at[spots[0]].set(low).at[spots[1]].set(top_value)


def setup_inputs(seed: int = 0) -> dict:
    splits = jax.random.split(jax.random.key(seed), 6)
    u_velocity = draw_u_velocity(jax.random.fold_in(splits[5], 71), 0)
    v_velocity = draw_v_velocity(jax.random.fold_in(splits[5], 71), 0)
    ocean_mask = draw_ocean_mask(jax.random.fold_in(splits[5], 71), 0)
    tile_owner = draw_tile_owner(jax.random.fold_in(splits[5], 71), 0)
    lower_edge_quarter_turns = with_ends(jax.random.randint(splits[4], (N_TILE,), 0, 4), jax.random.fold_in(splits[4], 1), 0, 3).astype(jnp.int32)
    return {"u_velocity": u_velocity, "v_velocity": v_velocity, "ocean_mask": ocean_mask, "tile_owner": tile_owner, "lower_edge_quarter_turns": lower_edge_quarter_turns}


KAPPA = 0.2


def quarter(first, second, turns):
    cosine = jnp.where(turns == 0, 1.0, jnp.where(turns == 2, -1.0, 0.0)).astype(first.dtype)
    sine = jnp.where(turns == 1, 1.0, jnp.where(turns == 3, -1.0, 0.0)).astype(first.dtype)
    return cosine * first - sine * second, sine * first + cosine * second


def neighbours(u_field, v_field, lower_edge_quarter_turns, block_rows):
    total = u_field.shape[0]
    index = jnp.arange(total, dtype=jnp.int32)
    block = index // block_rows
    blocks = total // block_rows
    zero_turn = jnp.zeros((total,), jnp.int32)
    k_up = jnp.where(index % block_rows == 0, lower_edge_quarter_turns[block], zero_turn)[:, None]
    k_down = jnp.where(index % block_rows == block_rows - 1, (4 - lower_edge_quarter_turns[(block + 1) % blocks]) % 4, zero_turn)[:, None]
    above = quarter(jnp.roll(u_field, 1, 0), jnp.roll(v_field, 1, 0), k_up)
    below = quarter(jnp.roll(u_field, -1, 0), jnp.roll(v_field, -1, 0), k_down)
    left_pair = (jnp.roll(u_field, 1, 1), jnp.roll(v_field, 1, 1))
    right_pair = (jnp.roll(u_field, -1, 1), jnp.roll(v_field, -1, 1))
    return above, below, left_pair, right_pair


def make_terms(u_part, v_part, vort, strain, stretch):
    listed = [u_part, v_part, vort, strain, stretch, vort * vort, vort * strain, vort * stretch,
              strain * strain, stretch * stretch, strain * stretch, u_part * vort, v_part * vort,
              u_part * strain, v_part * stretch, u_part * v_part]
    return jnp.stack(listed, axis=-2)


def tiled(field):
    shaped = field.reshape(N_TILE, GX, TS, N_COL, GY, TS)
    shaped = jnp.transpose(shaped, (0, 3, 1, 4, 2, 5))
    return shaped.reshape(N_TILE, N_COL, TPD, TC)


def reference(u_velocity, v_velocity, ocean_mask, tile_owner, lower_edge_quarter_turns):
    u_field, v_field = u_velocity, v_velocity
    for step in range(PASSES):
        above, below, left_pair, right_pair = neighbours(u_field, v_field, lower_edge_quarter_turns, CX)
        following_u_velocity = u_field + KAPPA * (above[0] + below[0] + left_pair[0] + right_pair[0] - 4.0 * u_field)
        v_next = v_field + KAPPA * (above[1] + below[1] + left_pair[1] + right_pair[1] - 4.0 * v_field)
        u_field, v_field = following_u_velocity, v_next
    coarse_u = u_field.reshape(NX // 4, 4, NY // 4, 4).mean(axis=(1, 3))
    coarse_v = v_field.reshape(NX // 4, 4, NY // 4, 4).mean(axis=(1, 3))
    above, below, left_pair, right_pair = neighbours(coarse_u, coarse_v, lower_edge_quarter_turns, CX // 4)
    u_dx = (right_pair[0] - left_pair[0]) * 0.5
    u_dy = (below[0] - above[0]) * 0.5
    v_dx = (right_pair[1] - left_pair[1]) * 0.5
    v_dy = (below[1] - above[1]) * 0.5
    vort = v_dx - u_dy
    strain = u_dy + v_dx
    stretch = u_dx - v_dy
    terms = make_terms(tiled(coarse_u), tiled(coarse_v), tiled(vort), tiled(strain), tiled(stretch))
    mask_tiles = jnp.transpose(ocean_mask.reshape(N_TILE, GX, N_COL, GY), (0, 2, 1, 3)).reshape(N_TILE, N_COL, TPD)
    owner_tiles = jnp.transpose(tile_owner.reshape(N_TILE, GX, N_COL, GY), (0, 2, 1, 3)).reshape(N_TILE, N_COL, TPD)
    live = mask_tiles == 1
    local = jnp.arange(TPD, dtype=jnp.int32)
    same = (owner_tiles[..., :, None] == owner_tiles[..., None, :]) & live[..., None, :] & (local[None, :] < local[:, None])
    slot = jnp.sum(same.astype(jnp.int32), axis=-1)
    owners_all = jnp.arange(N_TILE, dtype=jnp.int32)
    slots_all = jnp.arange(CAP, dtype=jnp.int32)
    chosen_terms = (live[..., None, None] & (owner_tiles[..., None, None] == owners_all[:, None])
              & (slot[..., None, None] == slots_all[None, :])).astype(jnp.float32)
    library = jnp.einsum('sclop,sclnx->ocspnx', chosen_terms, terms, precision=lax.Precision.HIGHEST)
    library = library.reshape(N_TILE, N_COL, N_TILE * CAP, TERMS, TC)
    masked = terms * live.astype(jnp.float32)[..., None, None]
    gram = jnp.einsum('sclnx,sclmx->nm', masked, terms, precision=lax.Precision.HIGHEST)
    gram = gram / ((CX // 4) * (CY // 4))
    return library, gram
```

```python
import functools

import jax
import jax.numpy as jnp
from jax import lax
from jax.experimental import pallas as pl
from jax.experimental.pallas import tpu as pltpu
from jax.sharding import PartitionSpec as P

PASSES = 8
KAPPA = 0.2
TERMS = 16
LANES = 128
HALO = 16
MARGIN = 8
STEP = 112
PAIR = 2
MESH = pl.DeviceIdType.MESH


def lanes_of(shape):
    return lax.broadcasted_iota(jnp.int32, shape, len(shape) - 1)


def turn(first, second, turns):
    cosine = jnp.where(turns == 0, 1.0, jnp.where(turns == 2, -1.0, 0.0)).astype(jnp.float32)
    sine = jnp.where(turns == 1, 1.0, jnp.where(turns == 3, -1.0, 0.0)).astype(jnp.float32)
    return cosine * first - sine * second, sine * first + cosine * second


def make_terms(u_part, v_part, vort, strain, stretch):
    return [
        u_part, v_part, vort, strain, stretch, vort * vort, vort * strain, vort * stretch,
        strain * strain, stretch * stretch, strain * stretch, u_part * vort, v_part * vort,
        u_part * strain, v_part * stretch, u_part * v_part,
    ]


def kernel(n_tile, n_col, grid_x, grid_y, u_ref, v_ref, mask_ref, owner_ref, turns_ref,
           library_ref, gram_ref, strip_a, strip_b, weights, row_sums, centre, across, fields,
           tiles, terms, out_tiles, in_tiles, block_terms, pack, in_cols, in_rows, in_corners,
           gram_out, gram_in, gram_out2, gram_in2, pick, kept,
           halo_send, halo_recv, all_send, all_recv, sum_send, sum_recv, sum2_send, sum2_recv,
           own_sem):
    t = lax.axis_index("tile")
    c = lax.axis_index("col")
    up, down = lax.rem(t + n_tile - 1, n_tile), lax.rem(t + 1, n_tile)
    left, right = lax.rem(c + n_col - 1, n_col), lax.rem(c + 1, n_col)
    rows, cols = u_ref.shape
    count = grid_x * grid_y
    slots = count // n_tile
    inputs = (u_ref, v_ref)
    last = cols - LANES

    tile_peers = [(lax.rem(t + d, n_tile), c) for d in range(1, n_tile)]
    col_peers = [(t, lax.rem(c + d, n_col)) for d in range(1, n_col)]
    corners = [(up, left), (up, right), (down, left), (down, right)]
    barrier = pltpu.get_barrier_semaphore()
    everyone = tile_peers + col_peers + corners
    for peer in everyone:
        pl.semaphore_signal(barrier, inc=1, device_id=peer, device_id_type=MESH)

    group = rows // 8
    lane = lanes_of((group, LANES))
    for comp in range(PAIR):
        first = jnp.zeros((group, LANES), jnp.float32)
        final = jnp.zeros((group, LANES), jnp.float32)
        for j in range(8):
            here = (lane >= HALO * j) & (lane < HALO * (j + 1))
            block = inputs[comp][j * group:(j + 1) * group, :LANES]
            first = jnp.where(here, pltpu.roll(block, HALO * j, 1) if j else block, first)
            block = inputs[comp][j * group:(j + 1) * group, last:]
            final = jnp.where(here, pltpu.roll(block, HALO * (j + 1), 1) if j < 7 else block, final)
        pack[0, comp] = first
        pack[1, comp] = final

    pl.semaphore_wait(barrier, len(everyone))

    copies = []

    def send(src, dst, peer):
        k = len(copies)
        copy = pltpu.make_async_remote_copy(
            src_ref=src, dst_ref=dst, send_sem=halo_send.at[k], recv_sem=halo_recv.at[k],
            device_id=peer, device_id_type=MESH)
        copy.start()
        copies.append(copy)

    send(pack.at[1], in_cols.at[0], (t, right))
    send(pack.at[0], in_cols.at[1], (t, left))
    for comp in range(PAIR):
        send(inputs[comp].at[pl.ds(rows - HALO, HALO), :], in_rows.at[0, comp], (down, c))
        send(inputs[comp].at[pl.ds(0, HALO), :], in_rows.at[1, comp], (up, c))
    for comp in range(PAIR):
        low = inputs[comp].at[pl.ds(rows - HALO, HALO), :]
        high = inputs[comp].at[pl.ds(0, HALO), :]
        send(low.at[:, pl.ds(last, LANES)], in_corners.at[0, comp], (down, right))
        send(low.at[:, pl.ds(0, LANES)], in_corners.at[1, comp], (down, left))
        send(high.at[:, pl.ds(last, LANES)], in_corners.at[2, comp], (up, right))
        send(high.at[:, pl.ds(0, LANES)], in_corners.at[3, comp], (up, left))

    for o in range(n_tile):
        seen = jnp.int32(0)
        chosen = [jnp.int32(0)] * slots
        for h in range(count):
            hit = (mask_ref[h // grid_y, h % grid_y] == 1) & (owner_ref[h // grid_y, h % grid_y] == o)
            for p in range(slots):
                chosen[p] = jnp.where(hit & (seen == p), h, chosen[p])
            seen = seen + jnp.where(hit, 1, 0)
        for p in range(slots):
            pick[o * slots + p] = chosen[p]
            kept[o * slots + p] = jnp.where(seen > p, 1.0, 0.0).astype(jnp.float32)

    strips = strip_a.shape[0] // PAIR
    for s in range(strips):
        spot = lax.broadcasted_iota(jnp.int32, (LANES, 2 * LANES), 0)
        cell = lax.broadcasted_iota(jnp.int32, (LANES, 2 * LANES), 1)
        from_col = (spot + (s * STEP - HALO)) >> 2
        valid = (spot >= PASSES) & (spot < LANES - PASSES)
        low_half = cell < LANES
        target = jnp.where(low_half, cell, cell - LANES)
        plus = jnp.where(low_half, target, target + 1) == from_col
        minus = (jnp.logical_not(low_half)) & (target - 1 == from_col)
        value = jnp.where(plus, 1.0, jnp.where(minus, -1.0, 0.0))
        weights[s * LANES:(s + 1) * LANES, :] = jnp.where(valid, value, 0.0).astype(jnp.bfloat16)
    row_sums[...] = jnp.zeros(row_sums.shape, jnp.float32)
    for job in range(PAIR * strips):
        edge = jnp.zeros((MARGIN, LANES), jnp.float32)
        total = strip_a.shape[1]
        strip_a[job, 0:MARGIN, :] = edge
        strip_a[job, total - MARGIN:total, :] = edge
        strip_b[job, 0:MARGIN, :] = edge
        strip_b[job, total - MARGIN:total, :] = edge

    def split_strips(x, height):
        lane = lanes_of((height, LANES))
        out = []
        for s in range(1, strips - 1):
            shift = HALO * (s + 1)
            out.append(jnp.where(lane < shift, pltpu.roll(x[s - 1], shift, 1), pltpu.roll(x[s], shift, 1)))
        return out

    def outer_strips(x0, x3, before, after, height):
        lane = lanes_of((height, LANES))
        return (jnp.where(lane < HALO, before, pltpu.roll(x0, HALO, 1)),
                jnp.where(lane < HALO * strips, pltpu.roll(x3, HALO * strips, 1), after))

    top = MARGIN + HALO
    chunk = 32
    for comp in range(PAIR):
        for r in range(0, rows, chunk):
            x = [inputs[comp][r:r + chunk, k * LANES:(k + 1) * LANES] for k in range(cols // LANES)]
            for s, value in enumerate(split_strips(x, chunk)):
                strip_a[comp * strips + s + 1, top + r:top + r + chunk, :] = value

    for copy in copies:
        copy.wait()

    for comp in range(PAIR):
        for j in range(8):
            before_all = in_cols[0, comp]
            after_all = in_cols[1, comp]
            before_all = pltpu.roll(before_all, LANES - HALO * j, 1) if j else before_all
            shift = (HALO * (strips - j)) % LANES
            after_all = pltpu.roll(after_all, shift, 1) if shift else after_all
            for r in range(0, group, chunk):
                at = j * group + r
                first, final = outer_strips(
                    inputs[comp][at:at + chunk, :LANES], inputs[comp][at:at + chunk, last:],
                    before_all[r:r + chunk], after_all[r:r + chunk], chunk)
                strip_a[comp * strips, top + at:top + at + chunk, :] = first
                strip_a[comp * strips + strips - 1, top + at:top + at + chunk, :] = final

    k_top = turns_ref[t]
    k_bottom = (4 - turns_ref[down]) & 3
    for side, turns, at in ((0, k_top, MARGIN), (1, k_bottom, top + rows)):
        pair = turn(in_rows[side, 0], in_rows[side, 1], turns)
        before = turn(in_corners[2 * side, 0], in_corners[2 * side, 1], turns)
        after = turn(in_corners[2 * side + 1, 0], in_corners[2 * side + 1, 1], turns)
        for comp in range(PAIR):
            x = [pair[comp][:, k * LANES:(k + 1) * LANES] for k in range(cols // LANES)]
            first, final = outer_strips(
                x[0], x[-1], pltpu.roll(before[comp], HALO, 1),
                pltpu.roll(after[comp], HALO * strips, 1), HALO)
            for s, value in enumerate([first] + split_strips(x, HALO) + [final]):
                strip_a[comp * strips + s, at:at + HALO, :] = value

    inner = rows + 2 * HALO

    def one_pass(src, dst, job):
        for r in range(MARGIN, MARGIN + inner, chunk):
            mid = src[job, r:r + chunk, :]
            around = src[job, r - 1:r - 1 + chunk, :] + src[job, r + 1:r + 1 + chunk, :]
            beside = pltpu.roll(mid, 1, 1) + pltpu.roll(mid, LANES - 1, 1)
            dst[job, r:r + chunk, :] = (mid + around) + beside

    def two_passes(_, job):
        one_pass(strip_a, strip_b, job)
        one_pass(strip_b, strip_a, job)
        return job

    def filter_strip(job, carry):
        lax.fori_loop(0, PASSES // 2, two_passes, job)
        return carry

    lax.fori_loop(0, PAIR * strips, filter_strip, 0)

    side_rows = rows // 4
    for comp in range(PAIR):
        for s in range(strips):
            job = comp * strips + s
            where = slice(s * LANES, (s + 1) * LANES)
            row_sums[comp, 8:8 + side_rows, where] = (
                (strip_a[job, pl.ds(top, side_rows, stride=4), :]
                 + strip_a[job, pl.ds(top + 1, side_rows, stride=4), :])
                + (strip_a[job, pl.ds(top + 2, side_rows, stride=4), :]
                   + strip_a[job, pl.ds(top + 3, side_rows, stride=4), :]))
            row_sums[comp, 7:8, where] = jnp.sum(strip_a[job, top - 4:top, :], axis=0, keepdims=True)
            row_sums[comp, 8 + side_rows:9 + side_rows, where] = jnp.sum(
                strip_a[job, top + rows:top + rows + 4, :], axis=0, keepdims=True)

    scale = KAPPA ** PASSES / 16.0
    for comp in range(PAIR):
        x = row_sums[comp]
        high = x.astype(jnp.bfloat16)
        rest = x - high.astype(jnp.float32)
        mid = rest.astype(jnp.bfloat16)
        low = (rest - mid.astype(jnp.float32)).astype(jnp.bfloat16)
        w = weights[...]
        z = (jnp.dot(low, w, preferred_element_type=jnp.float32)
             + jnp.dot(mid, w, preferred_element_type=jnp.float32)
             + jnp.dot(high, w, preferred_element_type=jnp.float32))
        centre[comp] = z[:, :LANES] * scale
        across[comp] = z[:, LANES:] * (0.5 * scale)

    for r in range(0, side_rows, chunk):
        u_dx = across[0, 8 + r:8 + r + chunk, :]
        v_dx = across[1, 8 + r:8 + r + chunk, :]
        u_dy = (centre[0, 9 + r:9 + r + chunk, :] - centre[0, 7 + r:7 + r + chunk, :]) * 0.5
        v_dy = (centre[1, 9 + r:9 + r + chunk, :] - centre[1, 7 + r:7 + r + chunk, :]) * 0.5
        fields[0, r:r + chunk, :] = centre[0, 8 + r:8 + r + chunk, :]
        fields[1, r:r + chunk, :] = centre[1, 8 + r:8 + r + chunk, :]
        fields[2, r:r + chunk, :] = v_dx - u_dy
        fields[3, r:r + chunk, :] = u_dy + v_dx
        fields[4, r:r + chunk, :] = u_dx - v_dy

    ts = side_rows // grid_x
    per = LANES // ts
    lane = lanes_of((8, LANES)) // ts
    for a in range(grid_x):
        live = [jnp.where(mask_ref[a, e] == 1, 1.0, 0.0).astype(jnp.float32) for e in range(grid_y)]
        for f in range(5):
            parts = [fields[f, pl.ds(a * ts + j, 8, stride=per), :] for j in range(per)]
            for e in range(grid_y):
                value = parts[e]
                for j in range(per):
                    if j != e:
                        value = jnp.where(lane == j, pltpu.roll(parts[j], ((j - e) * ts) % LANES, 1), value)
                tiles[a * grid_y + e, f] = value * live[e]

    for q in range(count):
        out_tiles[q // slots, q % slots] = tiles[pick[q]] * kept[q]

    sends = []
    for d in range(1, n_tile):
        peer = lax.rem(t + d, n_tile)
        copy = pltpu.make_async_remote_copy(
            src_ref=out_tiles.at[peer], dst_ref=in_tiles.at[t],
            send_sem=all_send.at[d], recv_sem=all_recv.at[d],
            device_id=(peer, c), device_id_type=MESH)
        copy.start()
        sends.append(copy)
    own = pltpu.make_async_copy(out_tiles.at[t], in_tiles.at[t], own_sem)
    own.start()

    def term_step(h, carry):
        base = tiles[h]
        for n, value in enumerate(make_terms(*[base[f] for f in range(5)])):
            terms[n, h] = value
        return carry

    lax.fori_loop(0, count, term_step, 0)
    gram_lane = lanes_of((TERMS, LANES))

    def gram_step(n, carry):
        mine = terms[n]
        sums = [jnp.sum(jnp.sum(mine * terms[m], axis=0), axis=0, keepdims=True) for m in range(TERMS)]
        column = jnp.sum(jnp.concatenate(sums, axis=0), axis=1, keepdims=True)
        return jnp.where(gram_lane == n, column, carry)

    part = lax.fori_loop(0, TERMS, gram_step, jnp.zeros((TERMS, LANES), jnp.float32))
    gram_out[...] = part
    gram_in[t] = part
    first_sums = []
    for d in range(1, n_tile):
        copy = pltpu.make_async_remote_copy(
            src_ref=gram_out, dst_ref=gram_in.at[t],
            send_sem=sum_send.at[d], recv_sem=sum_recv.at[d],
            device_id=(lax.rem(t + d, n_tile), c), device_id_type=MESH)
        copy.start()
        first_sums.append(copy)
    for copy in first_sums:
        copy.wait()
    part = jnp.sum(gram_in[...], axis=0)
    gram_out2[...] = part
    gram_in2[c] = part
    second_sums = []
    for d in range(1, n_col):
        copy = pltpu.make_async_remote_copy(
            src_ref=gram_out2, dst_ref=gram_in2.at[c],
            send_sem=sum2_send.at[d], recv_sem=sum2_recv.at[d],
            device_id=(t, lax.rem(c + d, n_col)), device_id_type=MESH)
        copy.start()
        second_sums.append(copy)

    own.wait()
    for copy in sends:
        copy.wait()

    def library_step(q, carry):
        base = in_tiles[q // slots, q % slots]
        for n, value in enumerate(make_terms(*[base[f] for f in range(5)])):
            block_terms[n * 8:(n + 1) * 8, :] = value
        for s in range(8):
            library_ref[0, 0, q, :, s * LANES:(s + 1) * LANES] = block_terms[pl.ds(s, TERMS, stride=8), :]
        return carry

    lax.fori_loop(0, count, library_step, 0)

    for copy in second_sums:
        copy.wait()
    gram = jnp.sum(gram_in2[...], axis=0) / (side_rows * side_rows)
    gram_ref[...] = gram[:, :TERMS]


def per_device(n_tile, n_col, u_velocity, v_velocity, ocean_mask, tile_owner, lower_edge_quarter_turns):
    rows, cols = u_velocity.shape
    grid_x, grid_y = ocean_mask.shape
    count = grid_x * grid_y
    slots = count // n_tile
    strips = cols // LANES + 1
    height = rows + 2 * HALO + 2 * MARGIN
    side_rows = rows // 4
    cells = (side_rows // grid_x) ** 2
    vmem = pl.BlockSpec(memory_space=pltpu.VMEM)
    smem = pl.BlockSpec(memory_space=pltpu.SMEM)
    f32 = jnp.float32
    return pl.pallas_call(
        functools.partial(kernel, n_tile, n_col, grid_x, grid_y),
        out_shape=(
            jax.ShapeDtypeStruct((1, 1, count, TERMS, cells), f32),
            jax.ShapeDtypeStruct((TERMS, TERMS), f32),
        ),
        in_specs=[vmem, vmem, smem, smem, smem],
        out_specs=(vmem, vmem),
        scratch_shapes=[
            pltpu.VMEM((PAIR * strips, height, LANES), f32),
            pltpu.VMEM((PAIR * strips, height, LANES), f32),
            pltpu.VMEM((strips * LANES, 2 * LANES), jnp.bfloat16),
            pltpu.VMEM((PAIR, side_rows + 16, strips * LANES), f32),
            pltpu.VMEM((PAIR, side_rows + 16, LANES), f32),
            pltpu.VMEM((PAIR, side_rows + 16, LANES), f32),
            pltpu.VMEM((5, side_rows, LANES), f32),
            pltpu.VMEM((count, 5, 8, LANES), f32),
            pltpu.VMEM((TERMS, count, 8, LANES), f32),
            pltpu.VMEM((n_tile, slots, 5, 8, LANES), f32),
            pltpu.VMEM((n_tile, slots, 5, 8, LANES), f32),
            pltpu.VMEM((TERMS * 8, LANES), f32),
            pltpu.VMEM((2, PAIR, rows // 8, LANES), f32),
            pltpu.VMEM((2, PAIR, rows // 8, LANES), f32),
            pltpu.VMEM((2, PAIR, HALO, cols), f32),
            pltpu.VMEM((4, PAIR, HALO, LANES), f32),
            pltpu.VMEM((TERMS, LANES), f32),
            pltpu.VMEM((n_tile, TERMS, LANES), f32),
            pltpu.VMEM((TERMS, LANES), f32),
            pltpu.VMEM((n_col, TERMS, LANES), f32),
            pltpu.SMEM((count,), jnp.int32),
            pltpu.SMEM((count,), f32),
            pltpu.SemaphoreType.DMA((14,)),
            pltpu.SemaphoreType.DMA((14,)),
            pltpu.SemaphoreType.DMA((n_tile,)),
            pltpu.SemaphoreType.DMA((n_tile,)),
            pltpu.SemaphoreType.DMA((n_tile,)),
            pltpu.SemaphoreType.DMA((n_tile,)),
            pltpu.SemaphoreType.DMA((n_col,)),
            pltpu.SemaphoreType.DMA((n_col,)),
            pltpu.SemaphoreType.DMA,
        ],
        compiler_params=pltpu.CompilerParams(
            collective_id=0, has_side_effects=True, vmem_limit_bytes=40 * 1024 * 1024),
    )(u_velocity, v_velocity, ocean_mask, tile_owner, lower_edge_quarter_turns)


def solution(mesh):
    in_specs = (P("tile", "col"), P("tile", "col"), P("tile", "col"), P("tile", "col"), P())
    out_specs = (P("tile", "col", None, None, None), P())
    return jax.shard_map(
        functools.partial(per_device, mesh.shape["tile"], mesh.shape["col"]),
        mesh=mesh, in_specs=in_specs, out_specs=out_specs, check_vma=False,
    )
```

```python
import functools

import jax
import jax.numpy as jnp
from jax import lax
from jax.experimental import pallas as pl
from jax.experimental.pallas import tpu as pltpu
from jax.sharding import PartitionSpec as P

PASSES = 8
KAPPA = 0.2
TERMS = 16
LANES = 128
HALO = 16
STEP = 112
PAIR = 2
MESH = pl.DeviceIdType.MESH


def lanes_of(shape):
    return lax.broadcasted_iota(jnp.int32, shape, len(shape) - 1)


def turn(first, second, turns):
    cosine = jnp.where(turns == 0, 1.0, jnp.where(turns == 2, -1.0, 0.0)).astype(jnp.float32)
    sine = jnp.where(turns == 1, 1.0, jnp.where(turns == 3, -1.0, 0.0)).astype(jnp.float32)
    return cosine * first - sine * second, sine * first + cosine * second


def make_terms(u_part, v_part, vort, strain, stretch):
    return [
        u_part, v_part, vort, strain, stretch, vort * vort, vort * strain, vort * stretch,
        strain * strain, stretch * stretch, strain * stretch, u_part * vort, v_part * vort,
        u_part * strain, v_part * stretch, u_part * v_part,
    ]


def kernel(n_tile, n_col, grid_x, grid_y, u_hbm, v_hbm, mask_hbm, owner_hbm, turns_hbm,
           library_hbm, gram_ref, library_ref, inputs, mask_ref, owner_ref, turns_ref, strip_a, strip_b, strip_c,
           weights, row_sums, centre, across, fields,
           tiles, terms, products, out_tiles, in_tiles, block_terms, pack, in_cols, in_rows, in_corners,
           gram_out, gram_in, gram_out2, gram_in2, pick, kept, load_sem,
           halo_send, halo_recv, all_send, all_recv, sum_send, sum_recv, sum2_send, sum2_recv,
           own_sem, store_sem):
    t = lax.axis_index("tile")
    c = lax.axis_index("col")
    up, down = lax.rem(t + n_tile - 1, n_tile), lax.rem(t + 1, n_tile)
    left, right = lax.rem(c + n_col - 1, n_col), lax.rem(c + 1, n_col)
    rows, cols = u_hbm.shape
    count = grid_x * grid_y
    slots = count // n_tile
    sources = (u_hbm, v_hbm)
    last = cols - LANES
    blocks = cols // LANES

    tile_peers = [(lax.rem(t + d, n_tile), c) for d in range(1, n_tile)]
    col_peers = [(t, lax.rem(c + d, n_col)) for d in range(1, n_col)]
    corners = [(up, left), (up, right), (down, left), (down, right)]
    barrier = pltpu.get_barrier_semaphore()
    everyone = tile_peers + col_peers + corners
    for peer in everyone:
        pl.semaphore_signal(barrier, inc=1, device_id=peer, device_id_type=MESH)

    loads = []

    def load(src, dst):
        copy = pltpu.make_async_copy(src, dst, load_sem.at[len(loads)])
        copy.start()
        loads.append(copy)

    for k in [0, blocks - 1] + list(range(1, blocks - 1)):
        for comp in range(PAIR):
            load(sources[comp].at[:, pl.ds(k * LANES, LANES)], inputs.at[comp, k])
    load(mask_hbm, mask_ref)
    load(owner_hbm, owner_ref)
    load(turns_hbm, turns_ref)
    for copy in loads[:2 * PAIR]:
        copy.wait()

    group = rows // 8
    lane = lanes_of((group, LANES))
    for comp in range(PAIR):
        first = jnp.zeros((group, LANES), jnp.float32)
        final = jnp.zeros((group, LANES), jnp.float32)
        for j in range(8):
            here = (lane >= HALO * j) & (lane < HALO * (j + 1))
            block = inputs[comp, 0, j * group:(j + 1) * group, :]
            first = jnp.where(here, pltpu.roll(block, HALO * j, 1) if j else block, first)
            block = inputs[comp, blocks - 1, j * group:(j + 1) * group, :]
            final = jnp.where(here, pltpu.roll(block, HALO * (j + 1), 1) if j < 7 else block, final)
        pack[0, comp] = first
        pack[1, comp] = final

    pl.semaphore_wait(barrier, len(everyone))

    copies = []

    def send(src, dst, peer):
        k = len(copies)
        copy = pltpu.make_async_remote_copy(
            src_ref=src, dst_ref=dst, send_sem=halo_send.at[k], recv_sem=halo_recv.at[k],
            device_id=peer, device_id_type=MESH)
        copy.start()
        copies.append(copy)

    send(pack.at[1], in_cols.at[0], (t, right))
    send(pack.at[0], in_cols.at[1], (t, left))
    for comp in range(PAIR):
        send(sources[comp].at[pl.ds(rows - HALO, HALO), :], in_rows.at[0, comp], (down, c))
        send(sources[comp].at[pl.ds(0, HALO), :], in_rows.at[1, comp], (up, c))
    for comp in range(PAIR):
        low = sources[comp].at[pl.ds(rows - HALO, HALO), :]
        high = sources[comp].at[pl.ds(0, HALO), :]
        send(low.at[:, pl.ds(last, LANES)], in_corners.at[0, comp], (down, right))
        send(low.at[:, pl.ds(0, LANES)], in_corners.at[1, comp], (down, left))
        send(high.at[:, pl.ds(last, LANES)], in_corners.at[2, comp], (up, right))
        send(high.at[:, pl.ds(0, LANES)], in_corners.at[3, comp], (up, left))

    for copy in loads[2 * PAIR:]:
        copy.wait()

    for o in range(n_tile):
        seen = jnp.int32(0)
        chosen = [jnp.int32(0)] * slots
        for h in range(count):
            hit = (mask_ref[h // grid_y, h % grid_y] == 1) & (owner_ref[h // grid_y, h % grid_y] == o)
            for p in range(slots):
                chosen[p] = jnp.where(hit & (seen == p), h, chosen[p])
            seen = seen + jnp.where(hit, 1, 0)
        for p in range(slots):
            pick[o * slots + p] = chosen[p]
            kept[o * slots + p] = jnp.where(seen > p, 1.0, 0.0).astype(jnp.float32)

    strips = strip_a.shape[0] // PAIR
    for s in range(strips):
        spot = lax.broadcasted_iota(jnp.int32, (LANES, 2 * LANES), 0)
        cell = lax.broadcasted_iota(jnp.int32, (LANES, 2 * LANES), 1)
        from_col = (spot + (s * STEP - HALO)) >> 2
        valid = (spot >= PASSES) & (spot < LANES - PASSES)
        low_half = cell < LANES
        target = jnp.where(low_half, cell, cell - LANES)
        plus = jnp.where(low_half, target, target + 1) == from_col
        minus = (jnp.logical_not(low_half)) & (target - 1 == from_col)
        value = jnp.where(plus, 1.0, jnp.where(minus, -1.0, 0.0))
        weights[s * LANES:(s + 1) * LANES, :] = jnp.where(valid, value, 0.0).astype(jnp.bfloat16)
    def split_strips(x, height):
        lane = lanes_of((height, LANES))
        out = []
        for s in range(1, strips - 1):
            shift = HALO * (s + 1)
            out.append(jnp.where(lane < shift, pltpu.roll(x[s - 1], shift, 1), pltpu.roll(x[s], shift, 1)))
        return out

    def outer_strips(x0, x3, before, after, height):
        lane = lanes_of((height, LANES))
        return (jnp.where(lane < HALO, before, pltpu.roll(x0, HALO, 1)),
                jnp.where(lane < HALO * strips, pltpu.roll(x3, HALO * strips, 1), after))

    top = HALO
    chunk = 32
    for comp in range(PAIR):
        for r in range(0, rows, chunk):
            x = [inputs[comp, k, r:r + chunk, :] for k in range(blocks)]
            for s, value in enumerate(split_strips(x, chunk)):
                strip_a[comp * strips + s + 1, top + r:top + r + chunk, :] = value

    for copy in copies:
        copy.wait()

    for comp in range(PAIR):
        for j in range(8):
            before_all = in_cols[0, comp]
            after_all = in_cols[1, comp]
            before_all = pltpu.roll(before_all, LANES - HALO * j, 1) if j else before_all
            shift = (HALO * (strips - j)) % LANES
            after_all = pltpu.roll(after_all, shift, 1) if shift else after_all
            for r in range(0, group, chunk):
                at = j * group + r
                first, final = outer_strips(
                    inputs[comp, 0, at:at + chunk, :], inputs[comp, blocks - 1, at:at + chunk, :],
                    before_all[r:r + chunk], after_all[r:r + chunk], chunk)
                strip_a[comp * strips, top + at:top + at + chunk, :] = first
                strip_a[comp * strips + strips - 1, top + at:top + at + chunk, :] = final

    k_top = turns_ref[t]
    k_bottom = (4 - turns_ref[down]) & 3
    for side, turns, at in ((0, k_top, 0), (1, k_bottom, top + rows)):
        pair = turn(in_rows[side, 0], in_rows[side, 1], turns)
        before = turn(in_corners[2 * side, 0], in_corners[2 * side, 1], turns)
        after = turn(in_corners[2 * side + 1, 0], in_corners[2 * side + 1, 1], turns)
        for comp in range(PAIR):
            x = [pair[comp][:, k * LANES:(k + 1) * LANES] for k in range(cols // LANES)]
            first, final = outer_strips(
                x[0], x[-1], pltpu.roll(before[comp], HALO, 1),
                pltpu.roll(after[comp], HALO * strips, 1), HALO)
            for s, value in enumerate([first] + split_strips(x, HALO) + [final]):
                strip_a[comp * strips + s, at:at + HALO, :] = value

    depth = (rows + 2 * HALO) // 8

    def five(above, mid, below):
        return (mid + (above + below)) + (pltpu.roll(mid, 1, 1) + pltpu.roll(mid, LANES - 1, 1))

    def two_passes(fetch, emit):
        def get(k):
            if k < 0:
                return pltpu.roll(fetch(k + depth), 1, 0)
            if k >= depth:
                return pltpu.roll(fetch(k - depth), 7, 0)
            return fetch(k)

        x0, x1 = get(-2), get(-1)
        y0 = y1 = None
        for k in range(-1, depth + 1):
            x2 = get(k + 1)
            y2 = five(x0, x1, x2)
            if k >= 1:
                emit(k - 1, five(y0, y1, y2))
            x0, x1, y0, y1 = x1, x2, y1, y2

    def filter_strip(job, carry):
        def put(dst):
            def emit(k, value):
                dst[k * 8:(k + 1) * 8, :] = value
            return emit

        quad = []

        def emit_sums(k, value):
            quad.append(value)
            if len(quad) == 4:
                row_sums[job, pl.ds(k // 4, 8, stride=depth // 4), :] = (quad[0] + quad[1]) + (quad[2] + quad[3])
                quad.clear()

        two_passes(lambda k: strip_a[job, pl.ds(k, 8, stride=depth), :], put(strip_b))
        two_passes(lambda k: strip_b[k * 8:(k + 1) * 8, :], put(strip_c))
        two_passes(lambda k: strip_c[k * 8:(k + 1) * 8, :], put(strip_b))
        two_passes(lambda k: strip_b[k * 8:(k + 1) * 8, :], emit_sums)
        return carry

    lax.fori_loop(0, PAIR * strips, filter_strip, 0)

    side_rows = rows // 4
    edge = HALO // 4
    scale = KAPPA ** PASSES / 16.0
    for comp in range(PAIR):
        x = jnp.concatenate([row_sums[comp * strips + s] for s in range(strips)], axis=1)
        high = x.astype(jnp.bfloat16)
        rest = x - high.astype(jnp.float32)
        mid = rest.astype(jnp.bfloat16)
        low = (rest - mid.astype(jnp.float32)).astype(jnp.bfloat16)
        w = weights[...]
        z = (jnp.dot(low, w, preferred_element_type=jnp.float32)
             + jnp.dot(mid, w, preferred_element_type=jnp.float32)
             + jnp.dot(high, w, preferred_element_type=jnp.float32))
        centre[comp] = z[:, :LANES] * scale
        across[comp] = z[:, LANES:] * (0.5 * scale)

    for r in range(0, side_rows, chunk):
        u_dx = across[0, edge + r:edge + r + chunk, :]
        v_dx = across[1, edge + r:edge + r + chunk, :]
        u_dy = (centre[0, edge + 1 + r:edge + 1 + r + chunk, :] - centre[0, edge - 1 + r:edge - 1 + r + chunk, :]) * 0.5
        v_dy = (centre[1, edge + 1 + r:edge + 1 + r + chunk, :] - centre[1, edge - 1 + r:edge - 1 + r + chunk, :]) * 0.5
        fields[0, r:r + chunk, :] = centre[0, edge + r:edge + r + chunk, :]
        fields[1, r:r + chunk, :] = centre[1, edge + r:edge + r + chunk, :]
        fields[2, r:r + chunk, :] = v_dx - u_dy
        fields[3, r:r + chunk, :] = u_dy + v_dx
        fields[4, r:r + chunk, :] = u_dx - v_dy

    ts = side_rows // grid_x
    per = LANES // ts
    lane = lanes_of((8, LANES)) // ts
    for a in range(grid_x):
        live = [jnp.where(mask_ref[a, e] == 1, 1.0, 0.0).astype(jnp.float32) for e in range(grid_y)]
        for f in range(5):
            parts = [fields[f, pl.ds(a * ts + j, 8, stride=per), :] for j in range(per)]
            for e in range(grid_y):
                value = parts[e]
                for j in range(per):
                    if j != e:
                        value = jnp.where(lane == j, pltpu.roll(parts[j], ((j - e) * ts) % LANES, 1), value)
                tiles[a * grid_y + e, f] = value * live[e]

    for q in range(count):
        out_tiles[q // slots, q % slots] = tiles[pick[q]] * kept[q]

    sends = []
    for d in range(1, n_tile):
        peer = lax.rem(t + d, n_tile)
        copy = pltpu.make_async_remote_copy(
            src_ref=out_tiles.at[peer], dst_ref=in_tiles.at[t],
            send_sem=all_send.at[d], recv_sem=all_recv.at[d],
            device_id=(peer, c), device_id_type=MESH)
        copy.start()
        sends.append(copy)
    own = pltpu.make_async_copy(out_tiles.at[t], in_tiles.at[t], own_sem)
    own.start()

    def term_step(h, carry):
        base = tiles[h]
        for n, value in enumerate(make_terms(*[base[f] for f in range(5)])):
            terms[n, h] = value
        return carry

    lax.fori_loop(0, count, term_step, 0)

    def gram_step(n, carry):
        mine = terms[n]
        for m in range(TERMS):
            products[n, m * 8:(m + 1) * 8, :] = jnp.sum(mine * terms[m], axis=0)
        return carry

    lax.fori_loop(0, TERMS, gram_step, 0)
    gram_lane = lanes_of((TERMS, LANES))
    part = jnp.zeros((TERMS, LANES), jnp.float32)
    for n in range(TERMS):
        sums = products[n, pl.ds(0, TERMS, stride=8), :]
        for q in range(1, 8):
            sums = sums + products[n, pl.ds(q, TERMS, stride=8), :]
        part = jnp.where(gram_lane == n, jnp.sum(sums, axis=1, keepdims=True), part)
    gram_out[...] = part
    gram_in[t] = part
    first_sums = []
    for d in range(1, n_tile):
        copy = pltpu.make_async_remote_copy(
            src_ref=gram_out, dst_ref=gram_in.at[t],
            send_sem=sum_send.at[d], recv_sem=sum_recv.at[d],
            device_id=(lax.rem(t + d, n_tile), c), device_id_type=MESH)
        copy.start()
        first_sums.append(copy)

    def library_step(q, carry):
        base = in_tiles[q // slots, q % slots]
        for n, value in enumerate(make_terms(*[base[f] for f in range(5)])):
            block_terms[n * 8:(n + 1) * 8, :] = value
        for s in range(8):
            library_ref[q, :, s * LANES:(s + 1) * LANES] = block_terms[pl.ds(s, TERMS, stride=8), :]
        return carry

    own.wait()
    for copy in sends:
        copy.wait()
    half = count // 2
    stores = [
        pltpu.make_async_copy(library_ref.at[pl.ds(k * half, half)],
                              library_hbm.at[0, 0, pl.ds(k * half, half)], store_sem.at[k])
        for k in range(2)
    ]
    lax.fori_loop(0, half, library_step, 0)
    stores[0].start()

    for copy in first_sums:
        copy.wait()
    part = jnp.sum(gram_in[...], axis=0)
    gram_out2[...] = part
    gram_in2[c] = part
    second_sums = []
    for d in range(1, n_col):
        copy = pltpu.make_async_remote_copy(
            src_ref=gram_out2, dst_ref=gram_in2.at[c],
            send_sem=sum2_send.at[d], recv_sem=sum2_recv.at[d],
            device_id=(t, lax.rem(c + d, n_col)), device_id_type=MESH)
        copy.start()
        second_sums.append(copy)

    lax.fori_loop(half, count, library_step, 0)
    stores[1].start()
    for copy in second_sums:
        copy.wait()
    gram = jnp.sum(gram_in2[...], axis=0) / (side_rows * side_rows)
    gram_ref[...] = gram[:, :TERMS]
    for copy in stores:
        copy.wait()


def per_device(n_tile, n_col, u_velocity, v_velocity, ocean_mask, tile_owner, lower_edge_quarter_turns):
    rows, cols = u_velocity.shape
    grid_x, grid_y = ocean_mask.shape
    count = grid_x * grid_y
    slots = count // n_tile
    strips = cols // LANES + 1
    height = rows + 2 * HALO
    side_rows = rows // 4
    cells = (side_rows // grid_x) ** 2
    vmem = pl.BlockSpec(memory_space=pltpu.VMEM)
    hbm = pl.BlockSpec(memory_space=pltpu.HBM)
    f32 = jnp.float32
    return pl.pallas_call(
        functools.partial(kernel, n_tile, n_col, grid_x, grid_y),
        out_shape=(
            jax.ShapeDtypeStruct((1, 1, count, TERMS, cells), f32),
            jax.ShapeDtypeStruct((TERMS, TERMS), f32),
        ),
        in_specs=[hbm] * 5,
        out_specs=(hbm, vmem),
        scratch_shapes=[
            pltpu.VMEM((count, TERMS, cells), f32),
            pltpu.VMEM((PAIR, cols // LANES, rows, LANES), f32),
            pltpu.SMEM(ocean_mask.shape, jnp.int32),
            pltpu.SMEM(tile_owner.shape, jnp.int32),
            pltpu.SMEM(lower_edge_quarter_turns.shape, jnp.int32),
            pltpu.VMEM((PAIR * strips, height, LANES), f32),
            pltpu.VMEM((height, LANES), f32),
            pltpu.VMEM((height, LANES), f32),
            pltpu.VMEM((strips * LANES, 2 * LANES), jnp.bfloat16),
            pltpu.VMEM((PAIR * strips, height // 4, LANES), f32),
            pltpu.VMEM((PAIR, height // 4, LANES), f32),
            pltpu.VMEM((PAIR, height // 4, LANES), f32),
            pltpu.VMEM((5, side_rows, LANES), f32),
            pltpu.VMEM((count, 5, 8, LANES), f32),
            pltpu.VMEM((TERMS, count, 8, LANES), f32),
            pltpu.VMEM((TERMS, TERMS * 8, LANES), f32),
            pltpu.VMEM((n_tile, slots, 5, 8, LANES), f32),
            pltpu.VMEM((n_tile, slots, 5, 8, LANES), f32),
            pltpu.VMEM((TERMS * 8, LANES), f32),
            pltpu.VMEM((2, PAIR, rows // 8, LANES), f32),
            pltpu.VMEM((2, PAIR, rows // 8, LANES), f32),
            pltpu.VMEM((2, PAIR, HALO, cols), f32),
            pltpu.VMEM((4, PAIR, HALO, LANES), f32),
            pltpu.VMEM((TERMS, LANES), f32),
            pltpu.VMEM((n_tile, TERMS, LANES), f32),
            pltpu.VMEM((TERMS, LANES), f32),
            pltpu.VMEM((n_col, TERMS, LANES), f32),
            pltpu.SMEM((count,), jnp.int32),
            pltpu.SMEM((count,), f32),
            pltpu.SemaphoreType.DMA((PAIR * (cols // LANES) + 3,)),
            pltpu.SemaphoreType.DMA((14,)),
            pltpu.SemaphoreType.DMA((14,)),
            pltpu.SemaphoreType.DMA((n_tile,)),
            pltpu.SemaphoreType.DMA((n_tile,)),
            pltpu.SemaphoreType.DMA((n_tile,)),
            pltpu.SemaphoreType.DMA((n_tile,)),
            pltpu.SemaphoreType.DMA((n_col,)),
            pltpu.SemaphoreType.DMA((n_col,)),
            pltpu.SemaphoreType.DMA,
            pltpu.SemaphoreType.DMA((2,)),
        ],
        compiler_params=pltpu.CompilerParams(
            collective_id=0, has_side_effects=True, vmem_limit_bytes=60 * 1024 * 1024),
    )(u_velocity, v_velocity, ocean_mask, tile_owner, lower_edge_quarter_turns)


def solution(mesh):
    in_specs = (P("tile", "col"), P("tile", "col"), P("tile", "col"), P("tile", "col"), P())
    out_specs = (P("tile", "col", None, None, None), P())
    return jax.shard_map(
        functools.partial(per_device, mesh.shape["tile"], mesh.shape["col"]),
        mesh=mesh, in_specs=in_specs, out_specs=out_specs, check_vma=False,
    )
```

```python
import functools

import jax
import jax.numpy as jnp
from jax import lax
from jax.experimental import pallas as pl
from jax.experimental.pallas import tpu as pltpu
from jax.sharding import PartitionSpec as P

PASSES = 8
KAPPA = 0.2
TERMS = 16
LANES = 128
HALO = 16
STEP = 112
PAIR = 2
MESH = pl.DeviceIdType.MESH


def lanes_of(shape):
    return lax.broadcasted_iota(jnp.int32, shape, len(shape) - 1)


def turn(first, second, turns):
    cosine = jnp.where(turns == 0, 1.0, jnp.where(turns == 2, -1.0, 0.0)).astype(jnp.float32)
    sine = jnp.where(turns == 1, 1.0, jnp.where(turns == 3, -1.0, 0.0)).astype(jnp.float32)
    return cosine * first - sine * second, sine * first + cosine * second


def make_terms(u_part, v_part, vort, strain, stretch):
    return [
        u_part, v_part, vort, strain, stretch, vort * vort, vort * strain, vort * stretch,
        strain * strain, stretch * stretch, strain * stretch, u_part * vort, v_part * vort,
        u_part * strain, v_part * stretch, u_part * v_part,
    ]


def kernel(n_tile, n_col, grid_x, grid_y, u_hbm, v_hbm, mask_hbm, owner_hbm, turns_hbm,
           library_hbm, gram_ref, library_ref, inputs, mask_ref, owner_ref, turns_ref, strip_a, strip_b, strip_c,
           weights, row_sums, centre, across, fields,
           tiles, terms, products, out_tiles, in_tiles, block_terms, pack, in_cols, in_rows, in_corners,
           gram_out, gram_in, gram_out2, gram_in2, pick, kept, load_sem,
           halo_send, halo_recv, all_send, all_recv, sum_send, sum_recv, sum2_send, sum2_recv,
           own_sem, store_sem):
    t = lax.axis_index("tile")
    c = lax.axis_index("col")
    up, down = lax.rem(t + n_tile - 1, n_tile), lax.rem(t + 1, n_tile)
    left, right = lax.rem(c + n_col - 1, n_col), lax.rem(c + 1, n_col)
    rows, cols = u_hbm.shape
    count = grid_x * grid_y
    slots = count // n_tile
    sources = (u_hbm, v_hbm)
    last = cols - LANES
    blocks = cols // LANES

    tile_peers = [(lax.rem(t + d, n_tile), c) for d in range(1, n_tile)]
    col_peers = [(t, lax.rem(c + d, n_col)) for d in range(1, n_col)]
    corners = [(up, left), (up, right), (down, left), (down, right)]
    barrier = pltpu.get_barrier_semaphore()
    everyone = tile_peers + col_peers + corners
    for peer in everyone:
        pl.semaphore_signal(barrier, inc=1, device_id=peer, device_id_type=MESH)

    loads = []

    def load(src, dst):
        copy = pltpu.make_async_copy(src, dst, load_sem.at[len(loads)])
        copy.start()
        loads.append(copy)

    for k in [0, blocks - 1] + list(range(1, blocks - 1)):
        for comp in range(PAIR):
            load(sources[comp].at[:, pl.ds(k * LANES, LANES)], inputs.at[comp, k])
    load(mask_hbm, mask_ref)
    load(owner_hbm, owner_ref)
    load(turns_hbm, turns_ref)
    for copy in loads[:2 * PAIR]:
        copy.wait()

    group = rows // 8
    lane = lanes_of((group, LANES))
    for comp in range(PAIR):
        first = jnp.zeros((group, LANES), jnp.float32)
        final = jnp.zeros((group, LANES), jnp.float32)
        for j in range(8):
            here = (lane >= HALO * j) & (lane < HALO * (j + 1))
            block = inputs[comp, 0, j * group:(j + 1) * group, :]
            first = jnp.where(here, pltpu.roll(block, HALO * j, 1) if j else block, first)
            block = inputs[comp, blocks - 1, j * group:(j + 1) * group, :]
            final = jnp.where(here, pltpu.roll(block, HALO * (j + 1), 1) if j < 7 else block, final)
        pack[0, comp] = first
        pack[1, comp] = final

    pl.semaphore_wait(barrier, len(everyone))

    copies = []

    def send(src, dst, peer):
        k = len(copies)
        copy = pltpu.make_async_remote_copy(
            src_ref=src, dst_ref=dst, send_sem=halo_send.at[k], recv_sem=halo_recv.at[k],
            device_id=peer, device_id_type=MESH)
        copy.start()
        copies.append(copy)

    send(pack.at[1], in_cols.at[0], (t, right))
    send(pack.at[0], in_cols.at[1], (t, left))
    for comp in range(PAIR):
        send(sources[comp].at[pl.ds(rows - HALO, HALO), :], in_rows.at[0, comp], (down, c))
        send(sources[comp].at[pl.ds(0, HALO), :], in_rows.at[1, comp], (up, c))
    for comp in range(PAIR):
        low = sources[comp].at[pl.ds(rows - HALO, HALO), :]
        high = sources[comp].at[pl.ds(0, HALO), :]
        send(low.at[:, pl.ds(last, LANES)], in_corners.at[0, comp], (down, right))
        send(low.at[:, pl.ds(0, LANES)], in_corners.at[1, comp], (down, left))
        send(high.at[:, pl.ds(last, LANES)], in_corners.at[2, comp], (up, right))
        send(high.at[:, pl.ds(0, LANES)], in_corners.at[3, comp], (up, left))

    for copy in loads[2 * PAIR:]:
        copy.wait()

    for o in range(n_tile):
        seen = jnp.int32(0)
        chosen = [jnp.int32(0)] * slots
        for h in range(count):
            hit = (mask_ref[h // grid_y, h % grid_y] == 1) & (owner_ref[h // grid_y, h % grid_y] == o)
            for p in range(slots):
                chosen[p] = jnp.where(hit & (seen == p), h, chosen[p])
            seen = seen + jnp.where(hit, 1, 0)
        for p in range(slots):
            pick[o * slots + p] = chosen[p]
            kept[o * slots + p] = jnp.where(seen > p, 1.0, 0.0).astype(jnp.float32)

    strips = strip_a.shape[0] // PAIR
    for s in range(strips):
        spot = lax.broadcasted_iota(jnp.int32, (LANES, 2 * LANES), 0)
        cell = lax.broadcasted_iota(jnp.int32, (LANES, 2 * LANES), 1)
        from_col = (spot + (s * STEP - HALO)) >> 2
        valid = (spot >= PASSES) & (spot < LANES - PASSES)
        low_half = cell < LANES
        target = jnp.where(low_half, cell, cell - LANES)
        plus = jnp.where(low_half, target, target + 1) == from_col
        minus = (jnp.logical_not(low_half)) & (target - 1 == from_col)
        value = jnp.where(plus, 1.0, jnp.where(minus, -1.0, 0.0))
        weights[s * LANES:(s + 1) * LANES, :] = jnp.where(valid, value, 0.0).astype(jnp.bfloat16)
    def split_strips(x, height):
        lane = lanes_of((height, LANES))
        out = []
        for s in range(1, strips - 1):
            shift = HALO * (s + 1)
            out.append(jnp.where(lane < shift, pltpu.roll(x[s - 1], shift, 1), pltpu.roll(x[s], shift, 1)))
        return out

    def outer_strips(x0, x3, before, after, height):
        lane = lanes_of((height, LANES))
        return (jnp.where(lane < HALO, before, pltpu.roll(x0, HALO, 1)),
                jnp.where(lane < HALO * strips, pltpu.roll(x3, HALO * strips, 1), after))

    top = HALO
    chunk = 32
    for comp in range(PAIR):
        for r in range(0, rows, chunk):
            x = [inputs[comp, k, r:r + chunk, :] for k in range(blocks)]
            for s, value in enumerate(split_strips(x, chunk)):
                strip_a[comp * strips + s + 1, top + r:top + r + chunk, :] = value

    for copy in copies:
        copy.wait()

    for comp in range(PAIR):
        for j in range(8):
            before_all = in_cols[0, comp]
            after_all = in_cols[1, comp]
            before_all = pltpu.roll(before_all, LANES - HALO * j, 1) if j else before_all
            shift = (HALO * (strips - j)) % LANES
            after_all = pltpu.roll(after_all, shift, 1) if shift else after_all
            for r in range(0, group, chunk):
                at = j * group + r
                first, final = outer_strips(
                    inputs[comp, 0, at:at + chunk, :], inputs[comp, blocks - 1, at:at + chunk, :],
                    before_all[r:r + chunk], after_all[r:r + chunk], chunk)
                strip_a[comp * strips, top + at:top + at + chunk, :] = first
                strip_a[comp * strips + strips - 1, top + at:top + at + chunk, :] = final

    k_top = turns_ref[t]
    k_bottom = (4 - turns_ref[down]) & 3
    for side, turns, at in ((0, k_top, 0), (1, k_bottom, top + rows)):
        pair = turn(in_rows[side, 0], in_rows[side, 1], turns)
        before = turn(in_corners[2 * side, 0], in_corners[2 * side, 1], turns)
        after = turn(in_corners[2 * side + 1, 0], in_corners[2 * side + 1, 1], turns)
        for comp in range(PAIR):
            x = [pair[comp][:, k * LANES:(k + 1) * LANES] for k in range(cols // LANES)]
            first, final = outer_strips(
                x[0], x[-1], pltpu.roll(before[comp], HALO, 1),
                pltpu.roll(after[comp], HALO * strips, 1), HALO)
            for s, value in enumerate([first] + split_strips(x, HALO) + [final]):
                strip_a[comp * strips + s, at:at + HALO, :] = value

    depth = (rows + 2 * HALO) // 8

    step = 8 * 10
    inner = 8 * depth

    def wrap(dst):
        dst[0:8, :] = pltpu.roll(dst[inner:inner + 8, :], 1, 0)
        dst[inner + 8:inner + 16, :] = pltpu.roll(dst[8:16, :], 7, 0)

    def one_pass(src, dst):
        for r in range(8, 8 + inner, step):
            size = min(step, 8 + inner - r)
            mid = src[r:r + size, :]
            around = src[r - 8:r - 8 + size, :] + src[r + 8:r + 8 + size, :]
            beside = pltpu.roll(mid, 1, 1) + pltpu.roll(mid, LANES - 1, 1)
            dst[r:r + size, :] = (mid + around) + beside
        wrap(dst)

    def pass_pair(_, carry):
        one_pass(strip_b, strip_c)
        one_pass(strip_c, strip_b)
        return carry

    def filter_strip(job, carry):
        for k in range(depth):
            strip_b[(k + 1) * 8:(k + 2) * 8, :] = strip_a[job, pl.ds(k, 8, stride=depth), :]
        wrap(strip_b)
        lax.fori_loop(0, PASSES // 2, pass_pair, 0)
        for k in range(0, depth, 4):
            quad = [strip_b[(k + 1 + q) * 8:(k + 2 + q) * 8, :] for q in range(4)]
            row_sums[job, pl.ds(k // 4, 8, stride=depth // 4), :] = (quad[0] + quad[1]) + (quad[2] + quad[3])
        return carry

    lax.fori_loop(0, PAIR * strips, filter_strip, 0)

    side_rows = rows // 4
    edge = HALO // 4
    scale = KAPPA ** PASSES / 16.0
    for comp in range(PAIR):
        x = jnp.concatenate([row_sums[comp * strips + s] for s in range(strips)], axis=1)
        high = x.astype(jnp.bfloat16)
        rest = x - high.astype(jnp.float32)
        mid = rest.astype(jnp.bfloat16)
        low = (rest - mid.astype(jnp.float32)).astype(jnp.bfloat16)
        w = weights[...]
        z = (jnp.dot(low, w, preferred_element_type=jnp.float32)
             + jnp.dot(mid, w, preferred_element_type=jnp.float32)
             + jnp.dot(high, w, preferred_element_type=jnp.float32))
        centre[comp] = z[:, :LANES] * scale
        across[comp] = z[:, LANES:] * (0.5 * scale)

    for r in range(0, side_rows, chunk):
        u_dx = across[0, edge + r:edge + r + chunk, :]
        v_dx = across[1, edge + r:edge + r + chunk, :]
        u_dy = (centre[0, edge + 1 + r:edge + 1 + r + chunk, :] - centre[0, edge - 1 + r:edge - 1 + r + chunk, :]) * 0.5
        v_dy = (centre[1, edge + 1 + r:edge + 1 + r + chunk, :] - centre[1, edge - 1 + r:edge - 1 + r + chunk, :]) * 0.5
        fields[0, r:r + chunk, :] = centre[0, edge + r:edge + r + chunk, :]
        fields[1, r:r + chunk, :] = centre[1, edge + r:edge + r + chunk, :]
        fields[2, r:r + chunk, :] = v_dx - u_dy
        fields[3, r:r + chunk, :] = u_dy + v_dx
        fields[4, r:r + chunk, :] = u_dx - v_dy

    ts = side_rows // grid_x
    per = LANES // ts
    lane = lanes_of((8, LANES)) // ts
    for a in range(grid_x):
        live = [jnp.where(mask_ref[a, e] == 1, 1.0, 0.0).astype(jnp.float32) for e in range(grid_y)]
        for f in range(5):
            parts = [fields[f, pl.ds(a * ts + j, 8, stride=per), :] for j in range(per)]
            for e in range(grid_y):
                value = parts[e]
                for j in range(per):
                    if j != e:
                        value = jnp.where(lane == j, pltpu.roll(parts[j], ((j - e) * ts) % LANES, 1), value)
                tiles[a * grid_y + e, f] = value * live[e]

    for q in range(count):
        out_tiles[q // slots, q % slots] = tiles[pick[q]] * kept[q]

    sends = []
    for d in range(1, n_tile):
        peer = lax.rem(t + d, n_tile)
        copy = pltpu.make_async_remote_copy(
            src_ref=out_tiles.at[peer], dst_ref=in_tiles.at[t],
            send_sem=all_send.at[d], recv_sem=all_recv.at[d],
            device_id=(peer, c), device_id_type=MESH)
        copy.start()
        sends.append(copy)
    own = pltpu.make_async_copy(out_tiles.at[t], in_tiles.at[t], own_sem)
    own.start()

    def term_step(h, carry):
        base = tiles[h]
        for n, value in enumerate(make_terms(*[base[f] for f in range(5)])):
            terms[n, h] = value
        return carry

    lax.fori_loop(0, count, term_step, 0)

    def gram_step(n, carry):
        mine = terms[n]
        for m in range(TERMS):
            products[n, m * 8:(m + 1) * 8, :] = jnp.sum(mine * terms[m], axis=0)
        return carry

    lax.fori_loop(0, TERMS, gram_step, 0)
    gram_lane = lanes_of((TERMS, LANES))
    part = jnp.zeros((TERMS, LANES), jnp.float32)
    for n in range(TERMS):
        sums = products[n, pl.ds(0, TERMS, stride=8), :]
        for q in range(1, 8):
            sums = sums + products[n, pl.ds(q, TERMS, stride=8), :]
        part = jnp.where(gram_lane == n, jnp.sum(sums, axis=1, keepdims=True), part)
    gram_out[...] = part
    gram_in[t] = part
    first_sums = []
    for d in range(1, n_tile):
        copy = pltpu.make_async_remote_copy(
            src_ref=gram_out, dst_ref=gram_in.at[t],
            send_sem=sum_send.at[d], recv_sem=sum_recv.at[d],
            device_id=(lax.rem(t + d, n_tile), c), device_id_type=MESH)
        copy.start()
        first_sums.append(copy)

    def library_step(q, carry):
        base = in_tiles[q // slots, q % slots]
        for n, value in enumerate(make_terms(*[base[f] for f in range(5)])):
            block_terms[n * 8:(n + 1) * 8, :] = value
        for s in range(8):
            library_ref[q, :, s * LANES:(s + 1) * LANES] = block_terms[pl.ds(s, TERMS, stride=8), :]
        return carry

    own.wait()
    for copy in sends:
        copy.wait()
    half = count // 2
    stores = [
        pltpu.make_async_copy(library_ref.at[pl.ds(k * half, half)],
                              library_hbm.at[0, 0, pl.ds(k * half, half)], store_sem.at[k])
        for k in range(2)
    ]
    lax.fori_loop(0, half, library_step, 0)
    stores[0].start()

    for copy in first_sums:
        copy.wait()
    part = jnp.sum(gram_in[...], axis=0)
    gram_out2[...] = part
    gram_in2[c] = part
    second_sums = []
    for d in range(1, n_col):
        copy = pltpu.make_async_remote_copy(
            src_ref=gram_out2, dst_ref=gram_in2.at[c],
            send_sem=sum2_send.at[d], recv_sem=sum2_recv.at[d],
            device_id=(t, lax.rem(c + d, n_col)), device_id_type=MESH)
        copy.start()
        second_sums.append(copy)

    lax.fori_loop(half, count, library_step, 0)
    stores[1].start()
    for copy in second_sums:
        copy.wait()
    gram = jnp.sum(gram_in2[...], axis=0) / (side_rows * side_rows)
    gram_ref[...] = gram[:, :TERMS]
    for copy in stores:
        copy.wait()


def per_device(n_tile, n_col, u_velocity, v_velocity, ocean_mask, tile_owner, lower_edge_quarter_turns):
    rows, cols = u_velocity.shape
    grid_x, grid_y = ocean_mask.shape
    count = grid_x * grid_y
    slots = count // n_tile
    strips = cols // LANES + 1
    height = rows + 2 * HALO
    side_rows = rows // 4
    cells = (side_rows // grid_x) ** 2
    vmem = pl.BlockSpec(memory_space=pltpu.VMEM)
    hbm = pl.BlockSpec(memory_space=pltpu.HBM)
    f32 = jnp.float32
    return pl.pallas_call(
        functools.partial(kernel, n_tile, n_col, grid_x, grid_y),
        out_shape=(
            jax.ShapeDtypeStruct((1, 1, count, TERMS, cells), f32),
            jax.ShapeDtypeStruct((TERMS, TERMS), f32),
        ),
        in_specs=[hbm] * 5,
        out_specs=(hbm, vmem),
        scratch_shapes=[
            pltpu.VMEM((count, TERMS, cells), f32),
            pltpu.VMEM((PAIR, cols // LANES, rows, LANES), f32),
            pltpu.SMEM(ocean_mask.shape, jnp.int32),
            pltpu.SMEM(tile_owner.shape, jnp.int32),
            pltpu.SMEM(lower_edge_quarter_turns.shape, jnp.int32),
            pltpu.VMEM((PAIR * strips, height, LANES), f32),
            pltpu.VMEM((height + 16, LANES), f32),
            pltpu.VMEM((height + 16, LANES), f32),
            pltpu.VMEM((strips * LANES, 2 * LANES), jnp.bfloat16),
            pltpu.VMEM((PAIR * strips, height // 4, LANES), f32),
            pltpu.VMEM((PAIR, height // 4, LANES), f32),
            pltpu.VMEM((PAIR, height // 4, LANES), f32),
            pltpu.VMEM((5, side_rows, LANES), f32),
            pltpu.VMEM((count, 5, 8, LANES), f32),
            pltpu.VMEM((TERMS, count, 8, LANES), f32),
            pltpu.VMEM((TERMS, TERMS * 8, LANES), f32),
            pltpu.VMEM((n_tile, slots, 5, 8, LANES), f32),
            pltpu.VMEM((n_tile, slots, 5, 8, LANES), f32),
            pltpu.VMEM((TERMS * 8, LANES), f32),
            pltpu.VMEM((2, PAIR, rows // 8, LANES), f32),
            pltpu.VMEM((2, PAIR, rows // 8, LANES), f32),
            pltpu.VMEM((2, PAIR, HALO, cols), f32),
            pltpu.VMEM((4, PAIR, HALO, LANES), f32),
            pltpu.VMEM((TERMS, LANES), f32),
            pltpu.VMEM((n_tile, TERMS, LANES), f32),
            pltpu.VMEM((TERMS, LANES), f32),
            pltpu.VMEM((n_col, TERMS, LANES), f32),
            pltpu.SMEM((count,), jnp.int32),
            pltpu.SMEM((count,), f32),
            pltpu.SemaphoreType.DMA((PAIR * (cols // LANES) + 3,)),
            pltpu.SemaphoreType.DMA((14,)),
            pltpu.SemaphoreType.DMA((14,)),
            pltpu.SemaphoreType.DMA((n_tile,)),
            pltpu.SemaphoreType.DMA((n_tile,)),
            pltpu.SemaphoreType.DMA((n_tile,)),
            pltpu.SemaphoreType.DMA((n_tile,)),
            pltpu.SemaphoreType.DMA((n_col,)),
            pltpu.SemaphoreType.DMA((n_col,)),
            pltpu.SemaphoreType.DMA,
            pltpu.SemaphoreType.DMA((2,)),
        ],
        compiler_params=pltpu.CompilerParams(
            collective_id=0, has_side_effects=True, vmem_limit_bytes=60 * 1024 * 1024),
    )(u_velocity, v_velocity, ocean_mask, tile_owner, lower_edge_quarter_turns)


def solution(mesh):
    in_specs = (P("tile", "col"), P("tile", "col"), P("tile", "col"), P("tile", "col"), P())
    out_specs = (P("tile", "col", None, None, None), P())
    return jax.shard_map(
        functools.partial(per_device, mesh.shape["tile"], mesh.shape["col"]),
        mesh=mesh, in_specs=in_specs, out_specs=out_specs, check_vma=False,
    )
```

```python
import functools

import jax
import jax.numpy as jnp
from jax import lax
from jax.experimental import pallas as pl
from jax.experimental.pallas import tpu as pltpu
from jax.sharding import PartitionSpec as P

PASSES = 8
KAPPA = 0.2
TERMS = 16
LANES = 128
HALO = 16
PAIR = 2
MESH = pl.DeviceIdType.MESH


def lanes_of(shape):
    return lax.broadcasted_iota(jnp.int32, shape, len(shape) - 1)


def turn(first, second, turns):
    cosine = jnp.where(turns == 0, 1.0, jnp.where(turns == 2, -1.0, 0.0)).astype(jnp.float32)
    sine = jnp.where(turns == 1, 1.0, jnp.where(turns == 3, -1.0, 0.0)).astype(jnp.float32)
    return cosine * first - sine * second, sine * first + cosine * second


def make_terms(u_part, v_part, vort, strain, stretch):
    return [
        u_part, v_part, vort, strain, stretch, vort * vort, vort * strain, vort * stretch,
        strain * strain, stretch * stretch, strain * stretch, u_part * vort, v_part * vort,
        u_part * strain, v_part * stretch, u_part * v_part,
    ]


def kernel(n_tile, n_col, grid_x, grid_y, u_hbm, v_hbm, mask_hbm, owner_hbm, turns_hbm,
           library_hbm, gram_ref, library_ref, inputs, mask_ref, owner_ref, turns_ref, mixed, field_b, field_c,
           spread, weights, row_sums, centre, across, fields,
           tiles, terms, products, out_tiles, in_tiles, block_terms, pack, in_cols, in_rows, in_corners,
           gram_out, gram_in, gram_out2, gram_in2, pick, kept, load_sem,
           halo_send, halo_recv, all_send, all_recv, sum_send, sum_recv, sum2_send, sum2_recv,
           own_sem, store_sem):
    t = lax.axis_index("tile")
    c = lax.axis_index("col")
    up, down = lax.rem(t + n_tile - 1, n_tile), lax.rem(t + 1, n_tile)
    left, right = lax.rem(c + n_col - 1, n_col), lax.rem(c + 1, n_col)
    rows, cols = u_hbm.shape
    count = grid_x * grid_y
    slots = count // n_tile
    sources = (u_hbm, v_hbm)
    last = cols - LANES
    blocks = cols // LANES

    tile_peers = [(lax.rem(t + d, n_tile), c) for d in range(1, n_tile)]
    col_peers = [(t, lax.rem(c + d, n_col)) for d in range(1, n_col)]
    corners = [(up, left), (up, right), (down, left), (down, right)]
    barrier = pltpu.get_barrier_semaphore()
    everyone = tile_peers + col_peers + corners
    for peer in everyone:
        pl.semaphore_signal(barrier, inc=1, device_id=peer, device_id_type=MESH)

    loads = []

    def load(src, dst):
        copy = pltpu.make_async_copy(src, dst, load_sem.at[len(loads)])
        copy.start()
        loads.append(copy)

    for k in [0, blocks - 1] + list(range(1, blocks - 1)):
        for comp in range(PAIR):
            load(sources[comp].at[:, pl.ds(k * LANES, LANES)], inputs.at[comp, k])
    load(mask_hbm, mask_ref)
    load(owner_hbm, owner_ref)
    load(turns_hbm, turns_ref)
    for copy in loads[:2 * PAIR]:
        copy.wait()

    group = rows // 8
    lane = lanes_of((group, LANES))
    for comp in range(PAIR):
        first = jnp.zeros((group, LANES), jnp.float32)
        final = jnp.zeros((group, LANES), jnp.float32)
        for j in range(8):
            here = (lane >= HALO * j) & (lane < HALO * (j + 1))
            block = inputs[comp, 0, j * group:(j + 1) * group, :]
            first = jnp.where(here, pltpu.roll(block, HALO * j, 1) if j else block, first)
            block = inputs[comp, blocks - 1, j * group:(j + 1) * group, :]
            final = jnp.where(here, pltpu.roll(block, HALO * (j + 1), 1) if j < 7 else block, final)
        pack[0, comp] = first
        pack[1, comp] = final

    pl.semaphore_wait(barrier, len(everyone))

    copies = []

    def send(src, dst, peer):
        k = len(copies)
        copy = pltpu.make_async_remote_copy(
            src_ref=src, dst_ref=dst, send_sem=halo_send.at[k], recv_sem=halo_recv.at[k],
            device_id=peer, device_id_type=MESH)
        copy.start()
        copies.append(copy)

    send(pack.at[1], in_cols.at[0], (t, right))
    send(pack.at[0], in_cols.at[1], (t, left))
    for comp in range(PAIR):
        send(sources[comp].at[pl.ds(rows - HALO, HALO), :], in_rows.at[0, comp], (down, c))
        send(sources[comp].at[pl.ds(0, HALO), :], in_rows.at[1, comp], (up, c))
    for comp in range(PAIR):
        low = sources[comp].at[pl.ds(rows - HALO, HALO), :]
        high = sources[comp].at[pl.ds(0, HALO), :]
        send(low.at[:, pl.ds(last, LANES)], in_corners.at[0, comp], (down, right))
        send(low.at[:, pl.ds(0, LANES)], in_corners.at[1, comp], (down, left))
        send(high.at[:, pl.ds(last, LANES)], in_corners.at[2, comp], (up, right))
        send(high.at[:, pl.ds(0, LANES)], in_corners.at[3, comp], (up, left))

    for copy in loads[2 * PAIR:]:
        copy.wait()

    for o in range(n_tile):
        seen = jnp.int32(0)
        chosen = [jnp.int32(0)] * slots
        for h in range(count):
            hit = (mask_ref[h // grid_y, h % grid_y] == 1) & (owner_ref[h // grid_y, h % grid_y] == o)
            for p in range(slots):
                chosen[p] = jnp.where(hit & (seen == p), h, chosen[p])
            seen = seen + jnp.where(hit, 1, 0)
        for p in range(slots):
            pick[o * slots + p] = chosen[p]
            kept[o * slots + p] = jnp.where(seen > p, 1.0, 0.0).astype(jnp.float32)

    planes = blocks + 1
    spot = lax.broadcasted_iota(jnp.int32, (LANES, LANES), 0)
    cell = lax.broadcasted_iota(jnp.int32, (LANES, LANES), 1)
    for m in range(planes):
        column = cell * planes + m
        where = slice(m * LANES, (m + 1) * LANES)
        for k in range(blocks):
            spread[k * LANES:(k + 1) * LANES, where] = jnp.where(
                spot + (k * LANES + HALO) == column, 1.0, 0.0).astype(jnp.bfloat16)
        source = jnp.where(spot < HALO, spot, jnp.where(spot < 2 * HALO, spot + cols, -1))
        spread[cols:, where] = jnp.where(source == column, 1.0, 0.0).astype(jnp.bfloat16)
        from_col = (spot * planes + (m - HALO)) >> 2
        weights[where, :LANES] = jnp.where(from_col == cell, 1.0, 0.0).astype(jnp.bfloat16)
        weights[where, LANES:] = jnp.where(
            from_col == cell + 1, 1.0, jnp.where(from_col == cell - 1, -1.0, 0.0)).astype(jnp.bfloat16)

    def exact_dot(x, w):
        high = x.astype(jnp.bfloat16)
        low = (x - high.astype(jnp.float32)).astype(jnp.bfloat16)
        return (jnp.dot(low, w, preferred_element_type=jnp.float32)
                + jnp.dot(high, w, preferred_element_type=jnp.float32))

    top = HALO
    chunk = 32
    part_rows = 128

    def spread_rows(i, carry):
        comp, r = i // (rows // part_rows), (i % (rows // part_rows)) * part_rows
        r = pl.multiple_of(r, part_rows)
        x = jnp.concatenate([inputs[comp, k, pl.ds(r, part_rows), :] for k in range(blocks)], axis=1)
        y = exact_dot(x, spread[:cols, :])
        for m in range(planes):
            mixed[comp * planes + m, pl.ds(top + r, part_rows), :] = y[:, m * LANES:(m + 1) * LANES]
        return carry

    lax.fori_loop(0, PAIR * (rows // part_rows), spread_rows, 0)

    for copy in copies:
        copy.wait()

    def rim(before, after, height):
        lane = lanes_of((height, LANES))
        return jnp.where(lane < HALO, before, jnp.where(lane < 2 * HALO, after, 0.0))

    for comp in range(PAIR):
        rims = []
        for j in range(8):
            before, after = in_cols[0, comp], in_cols[1, comp]
            before = pltpu.roll(before, LANES - HALO * j, 1) if j else before
            shift = (HALO * (1 - j)) % LANES
            after = pltpu.roll(after, shift, 1) if shift else after
            rims.append(rim(before, after, group))
        for j in range(0, 8, 2):
            y = exact_dot(jnp.concatenate(rims[j:j + 2], axis=0), spread[cols:, :])
            for m in range(planes):
                at = slice(top + j * group, top + (j + 2) * group)
                mixed[comp * planes + m, at, :] += y[:, m * LANES:(m + 1) * LANES]

    k_top = turns_ref[t]
    k_bottom = (4 - turns_ref[down]) & 3
    for side, turns, at in ((0, k_top, 0), (1, k_bottom, top + rows)):
        pair = turn(in_rows[side, 0], in_rows[side, 1], turns)
        before = turn(in_corners[2 * side, 0], in_corners[2 * side, 1], turns)
        after = turn(in_corners[2 * side + 1, 0], in_corners[2 * side + 1, 1], turns)
        for comp in range(PAIR):
            ends = rim(pltpu.roll(before[comp], HALO, 1), pltpu.roll(after[comp], HALO, 1), HALO)
            y = exact_dot(jnp.concatenate([pair[comp], ends], axis=1), spread[...])
            for m in range(planes):
                mixed[comp * planes + m, at:at + HALO, :] = y[:, m * LANES:(m + 1) * LANES]

    depth = (rows + 2 * HALO) // 8

    inner = 8 * depth
    batch = depth // 4

    def wrap(dst):
        for m in range(planes):
            dst[m, 0:8, :] = pltpu.roll(dst[m, inner:inner + 8, :], 1, 0)
            dst[m, inner + 8:inner + 16, :] = pltpu.roll(dst[m, 8:16, :], 7, 0)

    def one_pass(src, dst):
        def line(k):
            return [src[m, k * 8:(k + 1) * 8, :] for m in range(planes)]

        for k0 in range(1, depth + 1, batch):
            lefts = [pltpu.roll(src[planes - 1, k * 8:(k + 1) * 8, :], 1, 1) for k in range(k0, k0 + batch)]
            rights = [pltpu.roll(src[0, k * 8:(k + 1) * 8, :], LANES - 1, 1) for k in range(k0, k0 + batch)]
            above, mid = line(k0 - 1), line(k0)
            for k in range(k0, k0 + batch):
                below = line(k + 1)
                beside = [lefts[k - k0]] + mid + [rights[k - k0]]
                for m in range(planes):
                    dst[m, k * 8:(k + 1) * 8, :] = (mid[m] + (above[m] + below[m])) + (beside[m] + beside[m + 2])
                above, mid = mid, below
        wrap(dst)

    def pass_pair(_, carry):
        one_pass(field_b, field_c)
        one_pass(field_c, field_b)
        return carry

    def filter_field(comp, carry):
        for m in range(planes):
            for k in range(depth):
                field_b[m, (k + 1) * 8:(k + 2) * 8, :] = mixed[comp * planes + m, pl.ds(k, 8, stride=depth), :]
        wrap(field_b)
        lax.fori_loop(0, PASSES // 2, pass_pair, 0)
        for m in range(planes):
            for k in range(0, depth, 4):
                quad = [field_b[m, (k + 1 + q) * 8:(k + 2 + q) * 8, :] for q in range(4)]
                row_sums[comp * planes + m, pl.ds(k // 4, 8, stride=depth // 4), :] = (
                    (quad[0] + quad[1]) + (quad[2] + quad[3]))
        return carry

    lax.fori_loop(0, PAIR, filter_field, 0)

    side_rows = rows // 4
    edge = HALO // 4
    scale = KAPPA ** PASSES / 16.0
    for comp in range(PAIR):
        x = jnp.concatenate([row_sums[comp * planes + s] for s in range(planes)], axis=1)
        high = x.astype(jnp.bfloat16)
        rest = x - high.astype(jnp.float32)
        mid = rest.astype(jnp.bfloat16)
        low = (rest - mid.astype(jnp.float32)).astype(jnp.bfloat16)
        w = weights[...]
        z = (jnp.dot(low, w, preferred_element_type=jnp.float32)
             + jnp.dot(mid, w, preferred_element_type=jnp.float32)
             + jnp.dot(high, w, preferred_element_type=jnp.float32))
        centre[comp] = z[:, :LANES] * scale
        across[comp] = z[:, LANES:] * (0.5 * scale)

    for r in range(0, side_rows, chunk):
        u_dx = across[0, edge + r:edge + r + chunk, :]
        v_dx = across[1, edge + r:edge + r + chunk, :]
        u_dy = (centre[0, edge + 1 + r:edge + 1 + r + chunk, :] - centre[0, edge - 1 + r:edge - 1 + r + chunk, :]) * 0.5
        v_dy = (centre[1, edge + 1 + r:edge + 1 + r + chunk, :] - centre[1, edge - 1 + r:edge - 1 + r + chunk, :]) * 0.5
        fields[0, r:r + chunk, :] = centre[0, edge + r:edge + r + chunk, :]
        fields[1, r:r + chunk, :] = centre[1, edge + r:edge + r + chunk, :]
        fields[2, r:r + chunk, :] = v_dx - u_dy
        fields[3, r:r + chunk, :] = u_dy + v_dx
        fields[4, r:r + chunk, :] = u_dx - v_dy

    ts = side_rows // grid_x
    per = LANES // ts
    lane = lanes_of((8, LANES)) // ts
    for a in range(grid_x):
        live = [jnp.where(mask_ref[a, e] == 1, 1.0, 0.0).astype(jnp.float32) for e in range(grid_y)]
        for f in range(5):
            parts = [fields[f, pl.ds(a * ts + j, 8, stride=per), :] for j in range(per)]
            for e in range(grid_y):
                value = parts[e]
                for j in range(per):
                    if j != e:
                        value = jnp.where(lane == j, pltpu.roll(parts[j], ((j - e) * ts) % LANES, 1), value)
                tiles[a * grid_y + e, f] = value * live[e]

    for q in range(count):
        out_tiles[q // slots, q % slots] = tiles[pick[q]] * kept[q]

    sends = []
    for d in range(1, n_tile):
        peer = lax.rem(t + d, n_tile)
        copy = pltpu.make_async_remote_copy(
            src_ref=out_tiles.at[peer], dst_ref=in_tiles.at[t],
            send_sem=all_send.at[d], recv_sem=all_recv.at[d],
            device_id=(peer, c), device_id_type=MESH)
        copy.start()
        sends.append(copy)
    own = pltpu.make_async_copy(out_tiles.at[t], in_tiles.at[t], own_sem)
    own.start()

    def term_step(h, carry):
        base = tiles[h]
        for n, value in enumerate(make_terms(*[base[f] for f in range(5)])):
            terms[n, h] = value
        return carry

    lax.fori_loop(0, count, term_step, 0)

    def gram_step(n, carry):
        mine = terms[n]
        for m in range(TERMS):
            products[n, m * 8:(m + 1) * 8, :] = jnp.sum(mine * terms[m], axis=0)
        return carry

    lax.fori_loop(0, TERMS, gram_step, 0)
    gram_lane = lanes_of((TERMS, LANES))
    part = jnp.zeros((TERMS, LANES), jnp.float32)
    for n in range(TERMS):
        sums = products[n, pl.ds(0, TERMS, stride=8), :]
        for q in range(1, 8):
            sums = sums + products[n, pl.ds(q, TERMS, stride=8), :]
        part = jnp.where(gram_lane == n, jnp.sum(sums, axis=1, keepdims=True), part)
    gram_out[...] = part
    gram_in[t] = part
    first_sums = []
    for d in range(1, n_tile):
        copy = pltpu.make_async_remote_copy(
            src_ref=gram_out, dst_ref=gram_in.at[t],
            send_sem=sum_send.at[d], recv_sem=sum_recv.at[d],
            device_id=(lax.rem(t + d, n_tile), c), device_id_type=MESH)
        copy.start()
        first_sums.append(copy)

    def library_step(q, carry):
        base = in_tiles[q // slots, q % slots]
        for n, value in enumerate(make_terms(*[base[f] for f in range(5)])):
            block_terms[n * 8:(n + 1) * 8, :] = value
        for s in range(8):
            library_ref[q, :, s * LANES:(s + 1) * LANES] = block_terms[pl.ds(s, TERMS, stride=8), :]
        return carry

    own.wait()
    for copy in sends:
        copy.wait()
    half = count // 2
    stores = [
        pltpu.make_async_copy(library_ref.at[pl.ds(k * half, half)],
                              library_hbm.at[0, 0, pl.ds(k * half, half)], store_sem.at[k])
        for k in range(2)
    ]
    lax.fori_loop(0, half, library_step, 0)
    stores[0].start()

    for copy in first_sums:
        copy.wait()
    part = jnp.sum(gram_in[...], axis=0)
    gram_out2[...] = part
    gram_in2[c] = part
    second_sums = []
    for d in range(1, n_col):
        copy = pltpu.make_async_remote_copy(
            src_ref=gram_out2, dst_ref=gram_in2.at[c],
            send_sem=sum2_send.at[d], recv_sem=sum2_recv.at[d],
            device_id=(t, lax.rem(c + d, n_col)), device_id_type=MESH)
        copy.start()
        second_sums.append(copy)

    lax.fori_loop(half, count, library_step, 0)
    stores[1].start()
    for copy in second_sums:
        copy.wait()
    gram = jnp.sum(gram_in2[...], axis=0) / (side_rows * side_rows)
    gram_ref[...] = gram[:, :TERMS]
    for copy in stores:
        copy.wait()


def per_device(n_tile, n_col, u_velocity, v_velocity, ocean_mask, tile_owner, lower_edge_quarter_turns):
    rows, cols = u_velocity.shape
    grid_x, grid_y = ocean_mask.shape
    count = grid_x * grid_y
    slots = count // n_tile
    planes = cols // LANES + 1
    height = rows + 2 * HALO
    side_rows = rows // 4
    cells = (side_rows // grid_x) ** 2
    vmem = pl.BlockSpec(memory_space=pltpu.VMEM)
    hbm = pl.BlockSpec(memory_space=pltpu.HBM)
    f32 = jnp.float32
    return pl.pallas_call(
        functools.partial(kernel, n_tile, n_col, grid_x, grid_y),
        out_shape=(
            jax.ShapeDtypeStruct((1, 1, count, TERMS, cells), f32),
            jax.ShapeDtypeStruct((TERMS, TERMS), f32),
        ),
        in_specs=[hbm] * 5,
        out_specs=(hbm, vmem),
        scratch_shapes=[
            pltpu.VMEM((count, TERMS, cells), f32),
            pltpu.VMEM((PAIR, cols // LANES, rows, LANES), f32),
            pltpu.SMEM(ocean_mask.shape, jnp.int32),
            pltpu.SMEM(tile_owner.shape, jnp.int32),
            pltpu.SMEM(lower_edge_quarter_turns.shape, jnp.int32),
            pltpu.VMEM((PAIR * planes, height, LANES), f32),
            pltpu.VMEM((planes, height + 16, LANES), f32),
            pltpu.VMEM((planes, height + 16, LANES), f32),
            pltpu.VMEM((planes * LANES, planes * LANES), jnp.bfloat16),
            pltpu.VMEM((planes * LANES, 2 * LANES), jnp.bfloat16),
            pltpu.VMEM((PAIR * planes, height // 4, LANES), f32),
            pltpu.VMEM((PAIR, height // 4, LANES), f32),
            pltpu.VMEM((PAIR, height // 4, LANES), f32),
            pltpu.VMEM((5, side_rows, LANES), f32),
            pltpu.VMEM((count, 5, 8, LANES), f32),
            pltpu.VMEM((TERMS, count, 8, LANES), f32),
            pltpu.VMEM((TERMS, TERMS * 8, LANES), f32),
            pltpu.VMEM((n_tile, slots, 5, 8, LANES), f32),
            pltpu.VMEM((n_tile, slots, 5, 8, LANES), f32),
            pltpu.VMEM((TERMS * 8, LANES), f32),
            pltpu.VMEM((2, PAIR, rows // 8, LANES), f32),
            pltpu.VMEM((2, PAIR, rows // 8, LANES), f32),
            pltpu.VMEM((2, PAIR, HALO, cols), f32),
            pltpu.VMEM((4, PAIR, HALO, LANES), f32),
            pltpu.VMEM((TERMS, LANES), f32),
            pltpu.VMEM((n_tile, TERMS, LANES), f32),
            pltpu.VMEM((TERMS, LANES), f32),
            pltpu.VMEM((n_col, TERMS, LANES), f32),
            pltpu.SMEM((count,), jnp.int32),
            pltpu.SMEM((count,), f32),
            pltpu.SemaphoreType.DMA((PAIR * (cols // LANES) + 3,)),
            pltpu.SemaphoreType.DMA((14,)),
            pltpu.SemaphoreType.DMA((14,)),
            pltpu.SemaphoreType.DMA((n_tile,)),
            pltpu.SemaphoreType.DMA((n_tile,)),
            pltpu.SemaphoreType.DMA((n_tile,)),
            pltpu.SemaphoreType.DMA((n_tile,)),
            pltpu.SemaphoreType.DMA((n_col,)),
            pltpu.SemaphoreType.DMA((n_col,)),
            pltpu.SemaphoreType.DMA,
            pltpu.SemaphoreType.DMA((2,)),
        ],
        compiler_params=pltpu.CompilerParams(
            collective_id=0, has_side_effects=True, vmem_limit_bytes=60 * 1024 * 1024),
    )(u_velocity, v_velocity, ocean_mask, tile_owner, lower_edge_quarter_turns)


def solution(mesh):
    in_specs = (P("tile", "col"), P("tile", "col"), P("tile", "col"), P("tile", "col"), P())
    out_specs = (P("tile", "col", None, None, None), P())
    return jax.shard_map(
        functools.partial(per_device, mesh.shape["tile"], mesh.shape["col"]),
        mesh=mesh, in_specs=in_specs, out_specs=out_specs, check_vma=False,
    )
```

```python
import functools

import jax
import jax.numpy as jnp
from jax import lax
from jax.experimental import pallas as pl
from jax.experimental.pallas import tpu as pltpu
from jax.sharding import PartitionSpec as P

PASSES = 8
KAPPA = 0.2
TERMS = 16
LANES = 128
HALO = 16
PAIR = 2
MESH = pl.DeviceIdType.MESH


def lanes_of(shape):
    return lax.broadcasted_iota(jnp.int32, shape, len(shape) - 1)


def turn(first, second, turns):
    cosine = jnp.where(turns == 0, 1.0, jnp.where(turns == 2, -1.0, 0.0)).astype(jnp.float32)
    sine = jnp.where(turns == 1, 1.0, jnp.where(turns == 3, -1.0, 0.0)).astype(jnp.float32)
    return cosine * first - sine * second, sine * first + cosine * second


def make_terms(u_part, v_part, vort, strain, stretch):
    return [
        u_part, v_part, vort, strain, stretch, vort * vort, vort * strain, vort * stretch,
        strain * strain, stretch * stretch, strain * stretch, u_part * vort, v_part * vort,
        u_part * strain, v_part * stretch, u_part * v_part,
    ]


def kernel(n_tile, n_col, grid_x, grid_y, u_hbm, v_hbm, mask_hbm, owner_hbm, turns_hbm,
           library_hbm, gram_ref, library_ref, inputs, mask_ref, owner_ref, turns_ref, mixed, field_b, field_c,
           spread, weights, row_sums, centre, across, fields,
           tiles, terms, products, out_tiles, in_tiles, block_terms, pack, in_cols, in_rows, in_corners,
           gram_out, gram_in, gram_out2, gram_in2, pick, kept, load_sem,
           halo_send, halo_recv, all_send, all_recv, sum_send, sum_recv, sum2_send, sum2_recv,
           own_sem, store_sem):
    t = lax.axis_index("tile")
    c = lax.axis_index("col")
    up, down = lax.rem(t + n_tile - 1, n_tile), lax.rem(t + 1, n_tile)
    left, right = lax.rem(c + n_col - 1, n_col), lax.rem(c + 1, n_col)
    rows, cols = u_hbm.shape
    count = grid_x * grid_y
    slots = count // n_tile
    sources = (u_hbm, v_hbm)
    last = cols - LANES
    blocks = cols // LANES

    tile_peers = [(lax.rem(t + d, n_tile), c) for d in range(1, n_tile)]
    col_peers = [(t, lax.rem(c + d, n_col)) for d in range(1, n_col)]
    corners = [(up, left), (up, right), (down, left), (down, right)]
    barrier = pltpu.get_barrier_semaphore()
    everyone = tile_peers + col_peers + corners
    for peer in everyone:
        pl.semaphore_signal(barrier, inc=1, device_id=peer, device_id_type=MESH)

    loads = []

    def load(src, dst):
        copy = pltpu.make_async_copy(src, dst, load_sem.at[len(loads)])
        copy.start()
        loads.append(copy)

    for k in [0, blocks - 1] + list(range(1, blocks - 1)):
        for comp in range(PAIR):
            load(sources[comp].at[:, pl.ds(k * LANES, LANES)], inputs.at[comp, k])
    load(mask_hbm, mask_ref)
    load(owner_hbm, owner_ref)
    load(turns_hbm, turns_ref)
    for copy in loads[:2 * PAIR]:
        copy.wait()

    group = rows // 8
    lane = lanes_of((group, LANES))
    for comp in range(PAIR):
        first = jnp.zeros((group, LANES), jnp.float32)
        final = jnp.zeros((group, LANES), jnp.float32)
        for j in range(8):
            here = (lane >= HALO * j) & (lane < HALO * (j + 1))
            block = inputs[comp, 0, j * group:(j + 1) * group, :]
            first = jnp.where(here, pltpu.roll(block, HALO * j, 1) if j else block, first)
            block = inputs[comp, blocks - 1, j * group:(j + 1) * group, :]
            final = jnp.where(here, pltpu.roll(block, HALO * (j + 1), 1) if j < 7 else block, final)
        pack[0, comp] = first
        pack[1, comp] = final

    pl.semaphore_wait(barrier, len(everyone))

    copies = []

    def send(src, dst, peer):
        k = len(copies)
        copy = pltpu.make_async_remote_copy(
            src_ref=src, dst_ref=dst, send_sem=halo_send.at[k], recv_sem=halo_recv.at[k],
            device_id=peer, device_id_type=MESH)
        copy.start()
        copies.append(copy)

    send(pack.at[1], in_cols.at[0], (t, right))
    send(pack.at[0], in_cols.at[1], (t, left))
    for comp in range(PAIR):
        send(sources[comp].at[pl.ds(rows - HALO, HALO), :], in_rows.at[0, comp], (down, c))
        send(sources[comp].at[pl.ds(0, HALO), :], in_rows.at[1, comp], (up, c))
    for comp in range(PAIR):
        low = sources[comp].at[pl.ds(rows - HALO, HALO), :]
        high = sources[comp].at[pl.ds(0, HALO), :]
        send(low.at[:, pl.ds(last, LANES)], in_corners.at[0, comp], (down, right))
        send(low.at[:, pl.ds(0, LANES)], in_corners.at[1, comp], (down, left))
        send(high.at[:, pl.ds(last, LANES)], in_corners.at[2, comp], (up, right))
        send(high.at[:, pl.ds(0, LANES)], in_corners.at[3, comp], (up, left))

    for copy in loads[2 * PAIR:]:
        copy.wait()

    for o in range(n_tile):
        seen = jnp.int32(0)
        chosen = [jnp.int32(0)] * slots
        for h in range(count):
            hit = (mask_ref[h // grid_y, h % grid_y] == 1) & (owner_ref[h // grid_y, h % grid_y] == o)
            for p in range(slots):
                chosen[p] = jnp.where(hit & (seen == p), h, chosen[p])
            seen = seen + jnp.where(hit, 1, 0)
        for p in range(slots):
            pick[o * slots + p] = chosen[p]
            kept[o * slots + p] = jnp.where(seen > p, 1.0, 0.0).astype(jnp.float32)

    planes = blocks + 1
    spot = lax.broadcasted_iota(jnp.int32, (LANES, LANES), 0)
    cell = lax.broadcasted_iota(jnp.int32, (LANES, LANES), 1)
    for m in range(planes):
        column = cell * planes + m
        where = slice(m * LANES, (m + 1) * LANES)
        for k in range(blocks):
            spread[k * LANES:(k + 1) * LANES, where] = jnp.where(
                spot + (k * LANES + HALO) == column, 1.0, 0.0).astype(jnp.bfloat16)
        source = jnp.where(spot < HALO, spot, jnp.where(spot < 2 * HALO, spot + cols, -1))
        spread[cols:, where] = jnp.where(source == column, 1.0, 0.0).astype(jnp.bfloat16)
        from_col = (spot * planes + (m - HALO)) >> 2
        weights[where, :LANES] = jnp.where(from_col == cell, 1.0, 0.0).astype(jnp.bfloat16)
        weights[where, LANES:] = jnp.where(
            from_col == cell + 1, 1.0, jnp.where(from_col == cell - 1, -1.0, 0.0)).astype(jnp.bfloat16)

    def exact_dot(x, w):
        high = x.astype(jnp.bfloat16)
        low = (x - high.astype(jnp.float32)).astype(jnp.bfloat16)
        both = jnp.dot(jnp.concatenate([high, low], axis=0), w, preferred_element_type=jnp.float32)
        return both[:x.shape[0]] + both[x.shape[0]:]

    top = HALO
    chunk = 32
    part_rows = 256

    def spread_rows(i, carry):
        comp, r = i // (rows // part_rows), (i % (rows // part_rows)) * part_rows
        r = pl.multiple_of(r, part_rows)
        x = jnp.concatenate([inputs[comp, k, pl.ds(r, part_rows), :] for k in range(blocks)], axis=1)
        y = exact_dot(x, spread[:cols, :])
        for m in range(planes):
            mixed[comp * planes + m, pl.ds(top + r, part_rows), :] = y[:, m * LANES:(m + 1) * LANES]
        return carry

    lax.fori_loop(0, PAIR * (rows // part_rows), spread_rows, 0)

    for copy in copies:
        copy.wait()

    def rim(before, after, height):
        lane = lanes_of((height, LANES))
        return jnp.where(lane < HALO, before, jnp.where(lane < 2 * HALO, after, 0.0))

    for comp in range(PAIR):
        rims = []
        for j in range(8):
            before, after = in_cols[0, comp], in_cols[1, comp]
            before = pltpu.roll(before, LANES - HALO * j, 1) if j else before
            shift = (HALO * (1 - j)) % LANES
            after = pltpu.roll(after, shift, 1) if shift else after
            rims.append(rim(before, after, group))
        for j in range(0, 8, 4):
            y = exact_dot(jnp.concatenate(rims[j:j + 4], axis=0), spread[cols:, :])
            for m in range(planes):
                at = slice(top + j * group, top + (j + 4) * group)
                mixed[comp * planes + m, at, :] += y[:, m * LANES:(m + 1) * LANES]

    k_top = turns_ref[t]
    k_bottom = (4 - turns_ref[down]) & 3
    halo_rows = []
    for side, turns in ((0, k_top), (1, k_bottom)):
        pair = turn(in_rows[side, 0], in_rows[side, 1], turns)
        before = turn(in_corners[2 * side, 0], in_corners[2 * side, 1], turns)
        after = turn(in_corners[2 * side + 1, 0], in_corners[2 * side + 1, 1], turns)
        for comp in range(PAIR):
            ends = rim(pltpu.roll(before[comp], HALO, 1), pltpu.roll(after[comp], HALO, 1), HALO)
            halo_rows.append(jnp.concatenate([pair[comp], ends], axis=1))
    y = exact_dot(jnp.concatenate(halo_rows, axis=0), spread[...])
    for k in range(2 * PAIR):
        at = (k // PAIR) * (top + rows)
        for m in range(planes):
            mixed[(k % PAIR) * planes + m, at:at + HALO, :] = y[k * HALO:(k + 1) * HALO, m * LANES:(m + 1) * LANES]

    depth = (rows + 2 * HALO) // 8

    inner = 8 * depth
    batch = depth // 4

    def wrap(dst):
        for m in range(planes):
            dst[m, 0:8, :] = pltpu.roll(dst[m, inner:inner + 8, :], 1, 0)
            dst[m, inner + 8:inner + 16, :] = pltpu.roll(dst[m, 8:16, :], 7, 0)

    def one_pass(src, dst):
        def line(k):
            return [src[m, k * 8:(k + 1) * 8, :] for m in range(planes)]

        for k0 in range(1, depth + 1, batch):
            lefts = [pltpu.roll(src[planes - 1, k * 8:(k + 1) * 8, :], 1, 1) for k in range(k0, k0 + batch)]
            rights = [pltpu.roll(src[0, k * 8:(k + 1) * 8, :], LANES - 1, 1) for k in range(k0, k0 + batch)]
            above, mid = line(k0 - 1), line(k0)
            for k in range(k0, k0 + batch):
                below = line(k + 1)
                beside = [lefts[k - k0]] + mid + [rights[k - k0]]
                for m in range(planes):
                    dst[m, k * 8:(k + 1) * 8, :] = (mid[m] + (above[m] + below[m])) + (beside[m] + beside[m + 2])
                above, mid = mid, below
        wrap(dst)

    def pass_pair(_, carry):
        one_pass(field_b, field_c)
        one_pass(field_c, field_b)
        return carry

    def filter_field(comp, carry):
        for m in range(planes):
            for k in range(depth):
                field_b[m, (k + 1) * 8:(k + 2) * 8, :] = mixed[comp * planes + m, pl.ds(k, 8, stride=depth), :]
        wrap(field_b)
        lax.fori_loop(0, PASSES // 2, pass_pair, 0)
        for m in range(planes):
            for k in range(0, depth, 4):
                quad = [field_b[m, (k + 1 + q) * 8:(k + 2 + q) * 8, :] for q in range(4)]
                row_sums[comp * planes + m, pl.ds(k // 4, 8, stride=depth // 4), :] = (
                    (quad[0] + quad[1]) + (quad[2] + quad[3]))
        return carry

    lax.fori_loop(0, PAIR, filter_field, 0)

    side_rows = rows // 4
    edge = HALO // 4
    scale = KAPPA ** PASSES / 16.0
    x = jnp.concatenate([
        jnp.concatenate([row_sums[comp * planes + m] for m in range(planes)], axis=1)
        for comp in range(PAIR)], axis=0)
    high = x.astype(jnp.bfloat16)
    rest = x - high.astype(jnp.float32)
    mid = rest.astype(jnp.bfloat16)
    low = (rest - mid.astype(jnp.float32)).astype(jnp.bfloat16)
    z = jnp.dot(jnp.concatenate([low, mid, high], axis=0), weights[...], preferred_element_type=jnp.float32)
    tall = x.shape[0]
    z = (z[:tall] + z[tall:2 * tall]) + z[2 * tall:]
    for comp in range(PAIR):
        here = z[comp * (tall // PAIR):(comp + 1) * (tall // PAIR)]
        centre[comp] = here[:, :LANES] * scale
        across[comp] = here[:, LANES:] * (0.5 * scale)

    for r in range(0, side_rows, chunk):
        u_dx = across[0, edge + r:edge + r + chunk, :]
        v_dx = across[1, edge + r:edge + r + chunk, :]
        u_dy = (centre[0, edge + 1 + r:edge + 1 + r + chunk, :] - centre[0, edge - 1 + r:edge - 1 + r + chunk, :]) * 0.5
        v_dy = (centre[1, edge + 1 + r:edge + 1 + r + chunk, :] - centre[1, edge - 1 + r:edge - 1 + r + chunk, :]) * 0.5
        fields[0, r:r + chunk, :] = centre[0, edge + r:edge + r + chunk, :]
        fields[1, r:r + chunk, :] = centre[1, edge + r:edge + r + chunk, :]
        fields[2, r:r + chunk, :] = v_dx - u_dy
        fields[3, r:r + chunk, :] = u_dy + v_dx
        fields[4, r:r + chunk, :] = u_dx - v_dy

    ts = side_rows // grid_x
    per = LANES // ts
    lane = lanes_of((8, LANES)) // ts
    for a in range(grid_x):
        live = [jnp.where(mask_ref[a, e] == 1, 1.0, 0.0).astype(jnp.float32) for e in range(grid_y)]
        for f in range(5):
            parts = [fields[f, pl.ds(a * ts + j, 8, stride=per), :] for j in range(per)]
            for e in range(grid_y):
                value = parts[e]
                for j in range(per):
                    if j != e:
                        value = jnp.where(lane == j, pltpu.roll(parts[j], ((j - e) * ts) % LANES, 1), value)
                tiles[a * grid_y + e, f] = value * live[e]

    for q in range(count):
        out_tiles[q // slots, q % slots] = tiles[pick[q]] * kept[q]

    sends = []
    for d in range(1, n_tile):
        peer = lax.rem(t + d, n_tile)
        copy = pltpu.make_async_remote_copy(
            src_ref=out_tiles.at[peer], dst_ref=in_tiles.at[t],
            send_sem=all_send.at[d], recv_sem=all_recv.at[d],
            device_id=(peer, c), device_id_type=MESH)
        copy.start()
        sends.append(copy)
    own = pltpu.make_async_copy(out_tiles.at[t], in_tiles.at[t], own_sem)
    own.start()

    def term_step(h, carry):
        base = tiles[h]
        for n, value in enumerate(make_terms(*[base[f] for f in range(5)])):
            terms[n, h] = value
        return carry

    lax.fori_loop(0, count, term_step, 0)

    def gram_step(n, carry):
        mine = terms[n]
        for m in range(TERMS):
            products[n, m * 8:(m + 1) * 8, :] = jnp.sum(mine * terms[m], axis=0)
        return carry

    lax.fori_loop(0, TERMS, gram_step, 0)
    gram_lane = lanes_of((TERMS, LANES))
    part = jnp.zeros((TERMS, LANES), jnp.float32)
    for n in range(TERMS):
        sums = products[n, pl.ds(0, TERMS, stride=8), :]
        for q in range(1, 8):
            sums = sums + products[n, pl.ds(q, TERMS, stride=8), :]
        part = jnp.where(gram_lane == n, jnp.sum(sums, axis=1, keepdims=True), part)
    gram_out[...] = part
    gram_in[t] = part
    first_sums = []
    for d in range(1, n_tile):
        copy = pltpu.make_async_remote_copy(
            src_ref=gram_out, dst_ref=gram_in.at[t],
            send_sem=sum_send.at[d], recv_sem=sum_recv.at[d],
            device_id=(lax.rem(t + d, n_tile), c), device_id_type=MESH)
        copy.start()
        first_sums.append(copy)

    def library_step(q, carry):
        base = in_tiles[q // slots, q % slots]
        for n, value in enumerate(make_terms(*[base[f] for f in range(5)])):
            block_terms[n * 8:(n + 1) * 8, :] = value
        for s in range(8):
            library_ref[q, :, s * LANES:(s + 1) * LANES] = block_terms[pl.ds(s, TERMS, stride=8), :]
        return carry

    own.wait()
    for copy in sends:
        copy.wait()
    half = count // 2
    stores = [
        pltpu.make_async_copy(library_ref.at[pl.ds(k * half, half)],
                              library_hbm.at[0, 0, pl.ds(k * half, half)], store_sem.at[k])
        for k in range(2)
    ]
    lax.fori_loop(0, half, library_step, 0)
    stores[0].start()

    for copy in first_sums:
        copy.wait()
    part = jnp.sum(gram_in[...], axis=0)
    gram_out2[...] = part
    gram_in2[c] = part
    second_sums = []
    for d in range(1, n_col):
        copy = pltpu.make_async_remote_copy(
            src_ref=gram_out2, dst_ref=gram_in2.at[c],
            send_sem=sum2_send.at[d], recv_sem=sum2_recv.at[d],
            device_id=(t, lax.rem(c + d, n_col)), device_id_type=MESH)
        copy.start()
        second_sums.append(copy)

    lax.fori_loop(half, count, library_step, 0)
    stores[1].start()
    for copy in second_sums:
        copy.wait()
    gram = jnp.sum(gram_in2[...], axis=0) / (side_rows * side_rows)
    gram_ref[...] = gram[:, :TERMS]
    for copy in stores:
        copy.wait()


def per_device(n_tile, n_col, u_velocity, v_velocity, ocean_mask, tile_owner, lower_edge_quarter_turns):
    rows, cols = u_velocity.shape
    grid_x, grid_y = ocean_mask.shape
    count = grid_x * grid_y
    slots = count // n_tile
    planes = cols // LANES + 1
    height = rows + 2 * HALO
    side_rows = rows // 4
    cells = (side_rows // grid_x) ** 2
    vmem = pl.BlockSpec(memory_space=pltpu.VMEM)
    hbm = pl.BlockSpec(memory_space=pltpu.HBM)
    f32 = jnp.float32
    return pl.pallas_call(
        functools.partial(kernel, n_tile, n_col, grid_x, grid_y),
        out_shape=(
            jax.ShapeDtypeStruct((1, 1, count, TERMS, cells), f32),
            jax.ShapeDtypeStruct((TERMS, TERMS), f32),
        ),
        in_specs=[hbm] * 5,
        out_specs=(hbm, vmem),
        scratch_shapes=[
            pltpu.VMEM((count, TERMS, cells), f32),
            pltpu.VMEM((PAIR, cols // LANES, rows, LANES), f32),
            pltpu.SMEM(ocean_mask.shape, jnp.int32),
            pltpu.SMEM(tile_owner.shape, jnp.int32),
            pltpu.SMEM(lower_edge_quarter_turns.shape, jnp.int32),
            pltpu.VMEM((PAIR * planes, height, LANES), f32),
            pltpu.VMEM((planes, height + 16, LANES), f32),
            pltpu.VMEM((planes, height + 16, LANES), f32),
            pltpu.VMEM((planes * LANES, planes * LANES), jnp.bfloat16),
            pltpu.VMEM((planes * LANES, 2 * LANES), jnp.bfloat16),
            pltpu.VMEM((PAIR * planes, height // 4, LANES), f32),
            pltpu.VMEM((PAIR, height // 4, LANES), f32),
            pltpu.VMEM((PAIR, height // 4, LANES), f32),
            pltpu.VMEM((5, side_rows, LANES), f32),
            pltpu.VMEM((count, 5, 8, LANES), f32),
            pltpu.VMEM((TERMS, count, 8, LANES), f32),
            pltpu.VMEM((TERMS, TERMS * 8, LANES), f32),
            pltpu.VMEM((n_tile, slots, 5, 8, LANES), f32),
            pltpu.VMEM((n_tile, slots, 5, 8, LANES), f32),
            pltpu.VMEM((TERMS * 8, LANES), f32),
            pltpu.VMEM((2, PAIR, rows // 8, LANES), f32),
            pltpu.VMEM((2, PAIR, rows // 8, LANES), f32),
            pltpu.VMEM((2, PAIR, HALO, cols), f32),
            pltpu.VMEM((4, PAIR, HALO, LANES), f32),
            pltpu.VMEM((TERMS, LANES), f32),
            pltpu.VMEM((n_tile, TERMS, LANES), f32),
            pltpu.VMEM((TERMS, LANES), f32),
            pltpu.VMEM((n_col, TERMS, LANES), f32),
            pltpu.SMEM((count,), jnp.int32),
            pltpu.SMEM((count,), f32),
            pltpu.SemaphoreType.DMA((PAIR * (cols // LANES) + 3,)),
            pltpu.SemaphoreType.DMA((14,)),
            pltpu.SemaphoreType.DMA((14,)),
            pltpu.SemaphoreType.DMA((n_tile,)),
            pltpu.SemaphoreType.DMA((n_tile,)),
            pltpu.SemaphoreType.DMA((n_tile,)),
            pltpu.SemaphoreType.DMA((n_tile,)),
            pltpu.SemaphoreType.DMA((n_col,)),
            pltpu.SemaphoreType.DMA((n_col,)),
            pltpu.SemaphoreType.DMA,
            pltpu.SemaphoreType.DMA((2,)),
        ],
        compiler_params=pltpu.CompilerParams(
            collective_id=0, has_side_effects=True, vmem_limit_bytes=60 * 1024 * 1024),
    )(u_velocity, v_velocity, ocean_mask, tile_owner, lower_edge_quarter_turns)


def solution(mesh):
    in_specs = (P("tile", "col"), P("tile", "col"), P("tile", "col"), P("tile", "col"), P())
    out_specs = (P("tile", "col", None, None, None), P())
    return jax.shard_map(
        functools.partial(per_device, mesh.shape["tile"], mesh.shape["col"]),
        mesh=mesh, in_specs=in_specs, out_specs=out_specs, check_vma=False,
    )
```

```python
import functools

import jax
import jax.numpy as jnp
from jax import lax
from jax.experimental import pallas as pl
from jax.experimental.pallas import tpu as pltpu
from jax.sharding import PartitionSpec as P

PASSES = 8
KAPPA = 0.2
TERMS = 16
LANES = 128
HALO = 16
PAIR = 2
MESH = pl.DeviceIdType.MESH


def lanes_of(shape):
    return lax.broadcasted_iota(jnp.int32, shape, len(shape) - 1)


def turn(first, second, turns):
    cosine = jnp.where(turns == 0, 1.0, jnp.where(turns == 2, -1.0, 0.0)).astype(jnp.float32)
    sine = jnp.where(turns == 1, 1.0, jnp.where(turns == 3, -1.0, 0.0)).astype(jnp.float32)
    return cosine * first - sine * second, sine * first + cosine * second


def make_terms(u_part, v_part, vort, strain, stretch):
    return [
        u_part, v_part, vort, strain, stretch, vort * vort, vort * strain, vort * stretch,
        strain * strain, stretch * stretch, strain * stretch, u_part * vort, v_part * vort,
        u_part * strain, v_part * stretch, u_part * v_part,
    ]


def kernel(n_tile, n_col, grid_x, grid_y, u_hbm, v_hbm, mask_hbm, owner_hbm, turns_hbm,
           in_tiles, gram_ref, inputs, mask_ref, owner_ref, turns_ref, mixed, field_b, field_c,
           spread, weights, row_sums, centre, across, fields,
           tiles, terms, products, out_tiles, pack, in_cols, in_rows, in_corners,
           gram_out, gram_in, gram_out2, gram_in2, pick, kept, load_sem,
           halo_send, halo_recv, all_send, all_recv, sum_send, sum_recv, sum2_send, sum2_recv,
           own_sem):
    t = lax.axis_index("tile")
    c = lax.axis_index("col")
    up, down = lax.rem(t + n_tile - 1, n_tile), lax.rem(t + 1, n_tile)
    left, right = lax.rem(c + n_col - 1, n_col), lax.rem(c + 1, n_col)
    rows, cols = u_hbm.shape
    count = grid_x * grid_y
    slots = count // n_tile
    sources = (u_hbm, v_hbm)
    last = cols - LANES
    blocks = cols // LANES

    tile_peers = [(lax.rem(t + d, n_tile), c) for d in range(1, n_tile)]
    col_peers = [(t, lax.rem(c + d, n_col)) for d in range(1, n_col)]
    corners = [(up, left), (up, right), (down, left), (down, right)]
    barrier = pltpu.get_barrier_semaphore()
    everyone = tile_peers + col_peers + corners
    for peer in everyone:
        pl.semaphore_signal(barrier, inc=1, device_id=peer, device_id_type=MESH)

    loads = []

    def load(src, dst):
        copy = pltpu.make_async_copy(src, dst, load_sem.at[len(loads)])
        copy.start()
        loads.append(copy)

    for k in [0, blocks - 1] + list(range(1, blocks - 1)):
        for comp in range(PAIR):
            load(sources[comp].at[:, pl.ds(k * LANES, LANES)], inputs.at[comp, k])
    load(mask_hbm, mask_ref)
    load(owner_hbm, owner_ref)
    load(turns_hbm, turns_ref)
    for copy in loads[:2 * PAIR]:
        copy.wait()

    group = rows // 8
    lane = lanes_of((group, LANES))
    for comp in range(PAIR):
        first = jnp.zeros((group, LANES), jnp.float32)
        final = jnp.zeros((group, LANES), jnp.float32)
        for j in range(8):
            here = (lane >= HALO * j) & (lane < HALO * (j + 1))
            block = inputs[comp, 0, j * group:(j + 1) * group, :]
            first = jnp.where(here, pltpu.roll(block, HALO * j, 1) if j else block, first)
            block = inputs[comp, blocks - 1, j * group:(j + 1) * group, :]
            final = jnp.where(here, pltpu.roll(block, HALO * (j + 1), 1) if j < 7 else block, final)
        pack[0, comp] = first
        pack[1, comp] = final

    pl.semaphore_wait(barrier, len(everyone))

    copies = []

    def send(src, dst, peer):
        k = len(copies)
        copy = pltpu.make_async_remote_copy(
            src_ref=src, dst_ref=dst, send_sem=halo_send.at[k], recv_sem=halo_recv.at[k],
            device_id=peer, device_id_type=MESH)
        copy.start()
        copies.append(copy)

    send(pack.at[1], in_cols.at[0], (t, right))
    send(pack.at[0], in_cols.at[1], (t, left))
    for comp in range(PAIR):
        send(sources[comp].at[pl.ds(rows - HALO, HALO), :], in_rows.at[0, comp], (down, c))
        send(sources[comp].at[pl.ds(0, HALO), :], in_rows.at[1, comp], (up, c))
    for comp in range(PAIR):
        low = sources[comp].at[pl.ds(rows - HALO, HALO), :]
        high = sources[comp].at[pl.ds(0, HALO), :]
        send(low.at[:, pl.ds(last, LANES)], in_corners.at[0, comp], (down, right))
        send(low.at[:, pl.ds(0, LANES)], in_corners.at[1, comp], (down, left))
        send(high.at[:, pl.ds(last, LANES)], in_corners.at[2, comp], (up, right))
        send(high.at[:, pl.ds(0, LANES)], in_corners.at[3, comp], (up, left))

    for copy in loads[2 * PAIR:]:
        copy.wait()

    for o in range(n_tile):
        seen = jnp.int32(0)
        chosen = [jnp.int32(0)] * slots
        for h in range(count):
            hit = (mask_ref[h // grid_y, h % grid_y] == 1) & (owner_ref[h // grid_y, h % grid_y] == o)
            for p in range(slots):
                chosen[p] = jnp.where(hit & (seen == p), h, chosen[p])
            seen = seen + jnp.where(hit, 1, 0)
        for p in range(slots):
            pick[o * slots + p] = chosen[p]
            kept[o * slots + p] = jnp.where(seen > p, 1.0, 0.0).astype(jnp.float32)

    planes = blocks + 1
    spot = lax.broadcasted_iota(jnp.int32, (LANES, LANES), 0)
    cell = lax.broadcasted_iota(jnp.int32, (LANES, LANES), 1)
    for m in range(planes):
        column = cell * planes + m
        where = slice(m * LANES, (m + 1) * LANES)
        for k in range(blocks):
            spread[k * LANES:(k + 1) * LANES, where] = jnp.where(
                spot + (k * LANES + HALO) == column, 1.0, 0.0).astype(jnp.bfloat16)
        source = jnp.where(spot < HALO, spot, jnp.where(spot < 2 * HALO, spot + cols, -1))
        spread[cols:, where] = jnp.where(source == column, 1.0, 0.0).astype(jnp.bfloat16)
        from_col = (spot * planes + (m - HALO)) >> 2
        weights[where, :LANES] = jnp.where(from_col == cell, 1.0, 0.0).astype(jnp.bfloat16)
        weights[where, LANES:] = jnp.where(
            from_col == cell + 1, 1.0, jnp.where(from_col == cell - 1, -1.0, 0.0)).astype(jnp.bfloat16)

    def exact_dot(x, w):
        high = x.astype(jnp.bfloat16)
        low = (x - high.astype(jnp.float32)).astype(jnp.bfloat16)
        both = jnp.dot(jnp.concatenate([high, low], axis=0), w, preferred_element_type=jnp.float32)
        return both[:x.shape[0]] + both[x.shape[0]:]

    top = HALO
    chunk = 32
    part_rows = 256

    def spread_rows(i, carry):
        comp, r = i // (rows // part_rows), (i % (rows // part_rows)) * part_rows
        r = pl.multiple_of(r, part_rows)
        x = jnp.concatenate([inputs[comp, k, pl.ds(r, part_rows), :] for k in range(blocks)], axis=1)
        y = exact_dot(x, spread[:cols, :])
        for m in range(planes):
            mixed[comp * planes + m, pl.ds(top + r, part_rows), :] = y[:, m * LANES:(m + 1) * LANES]
        return carry

    lax.fori_loop(0, PAIR * (rows // part_rows), spread_rows, 0)

    for copy in copies:
        copy.wait()

    def rim(before, after, height):
        lane = lanes_of((height, LANES))
        return jnp.where(lane < HALO, before, jnp.where(lane < 2 * HALO, after, 0.0))

    for comp in range(PAIR):
        rims = []
        for j in range(8):
            before, after = in_cols[0, comp], in_cols[1, comp]
            before = pltpu.roll(before, LANES - HALO * j, 1) if j else before
            shift = (HALO * (1 - j)) % LANES
            after = pltpu.roll(after, shift, 1) if shift else after
            rims.append(rim(before, after, group))
        for j in range(0, 8, 4):
            y = exact_dot(jnp.concatenate(rims[j:j + 4], axis=0), spread[cols:, :])
            for m in range(planes):
                at = slice(top + j * group, top + (j + 4) * group)
                mixed[comp * planes + m, at, :] += y[:, m * LANES:(m + 1) * LANES]

    k_top = turns_ref[t]
    k_bottom = (4 - turns_ref[down]) & 3
    halo_rows = []
    for side, turns in ((0, k_top), (1, k_bottom)):
        pair = turn(in_rows[side, 0], in_rows[side, 1], turns)
        before = turn(in_corners[2 * side, 0], in_corners[2 * side, 1], turns)
        after = turn(in_corners[2 * side + 1, 0], in_corners[2 * side + 1, 1], turns)
        for comp in range(PAIR):
            ends = rim(pltpu.roll(before[comp], HALO, 1), pltpu.roll(after[comp], HALO, 1), HALO)
            halo_rows.append(jnp.concatenate([pair[comp], ends], axis=1))
    y = exact_dot(jnp.concatenate(halo_rows, axis=0), spread[...])
    for k in range(2 * PAIR):
        at = (k // PAIR) * (top + rows)
        for m in range(planes):
            mixed[(k % PAIR) * planes + m, at:at + HALO, :] = y[k * HALO:(k + 1) * HALO, m * LANES:(m + 1) * LANES]

    depth = (rows + 2 * HALO) // 8

    inner = 8 * depth
    batch = depth // 4

    def wrap(dst):
        for m in range(planes):
            dst[m, 0:8, :] = pltpu.roll(dst[m, inner:inner + 8, :], 1, 0)
            dst[m, inner + 8:inner + 16, :] = pltpu.roll(dst[m, 8:16, :], 7, 0)

    def one_pass(src, dst):
        def line(k):
            return [src[m, k * 8:(k + 1) * 8, :] for m in range(planes)]

        for k0 in range(1, depth + 1, batch):
            lefts = [pltpu.roll(src[planes - 1, k * 8:(k + 1) * 8, :], 1, 1) for k in range(k0, k0 + batch)]
            rights = [pltpu.roll(src[0, k * 8:(k + 1) * 8, :], LANES - 1, 1) for k in range(k0, k0 + batch)]
            above, mid = line(k0 - 1), line(k0)
            for k in range(k0, k0 + batch):
                below = line(k + 1)
                beside = [lefts[k - k0]] + mid + [rights[k - k0]]
                for m in range(planes):
                    dst[m, k * 8:(k + 1) * 8, :] = (mid[m] + (above[m] + below[m])) + (beside[m] + beside[m + 2])
                above, mid = mid, below
        wrap(dst)

    def pass_pair(_, carry):
        one_pass(field_b, field_c)
        one_pass(field_c, field_b)
        return carry

    def filter_field(comp, carry):
        for m in range(planes):
            for k in range(depth):
                field_b[m, (k + 1) * 8:(k + 2) * 8, :] = mixed[comp * planes + m, pl.ds(k, 8, stride=depth), :]
        wrap(field_b)
        lax.fori_loop(0, PASSES // 2, pass_pair, 0)
        for m in range(planes):
            for k in range(0, depth, 4):
                quad = [field_b[m, (k + 1 + q) * 8:(k + 2 + q) * 8, :] for q in range(4)]
                row_sums[comp * planes + m, pl.ds(k // 4, 8, stride=depth // 4), :] = (
                    (quad[0] + quad[1]) + (quad[2] + quad[3]))
        return carry

    lax.fori_loop(0, PAIR, filter_field, 0)

    side_rows = rows // 4
    edge = HALO // 4
    scale = KAPPA ** PASSES / 16.0
    x = jnp.concatenate([
        jnp.concatenate([row_sums[comp * planes + m] for m in range(planes)], axis=1)
        for comp in range(PAIR)], axis=0)
    high = x.astype(jnp.bfloat16)
    rest = x - high.astype(jnp.float32)
    mid = rest.astype(jnp.bfloat16)
    low = (rest - mid.astype(jnp.float32)).astype(jnp.bfloat16)
    z = jnp.dot(jnp.concatenate([low, mid, high], axis=0), weights[...], preferred_element_type=jnp.float32)
    tall = x.shape[0]
    z = (z[:tall] + z[tall:2 * tall]) + z[2 * tall:]
    for comp in range(PAIR):
        here = z[comp * (tall // PAIR):(comp + 1) * (tall // PAIR)]
        centre[comp] = here[:, :LANES] * scale
        across[comp] = here[:, LANES:] * (0.5 * scale)

    for r in range(0, side_rows, chunk):
        u_dx = across[0, edge + r:edge + r + chunk, :]
        v_dx = across[1, edge + r:edge + r + chunk, :]
        u_dy = (centre[0, edge + 1 + r:edge + 1 + r + chunk, :] - centre[0, edge - 1 + r:edge - 1 + r + chunk, :]) * 0.5
        v_dy = (centre[1, edge + 1 + r:edge + 1 + r + chunk, :] - centre[1, edge - 1 + r:edge - 1 + r + chunk, :]) * 0.5
        fields[0, r:r + chunk, :] = centre[0, edge + r:edge + r + chunk, :]
        fields[1, r:r + chunk, :] = centre[1, edge + r:edge + r + chunk, :]
        fields[2, r:r + chunk, :] = v_dx - u_dy
        fields[3, r:r + chunk, :] = u_dy + v_dx
        fields[4, r:r + chunk, :] = u_dx - v_dy

    ts = side_rows // grid_x
    per = LANES // ts
    lane = lanes_of((8, LANES)) // ts
    for a in range(grid_x):
        live = [jnp.where(mask_ref[a, e] == 1, 1.0, 0.0).astype(jnp.float32) for e in range(grid_y)]
        for f in range(5):
            parts = [fields[f, pl.ds(a * ts + j, 8, stride=per), :] for j in range(per)]
            for e in range(grid_y):
                value = parts[e]
                for j in range(per):
                    if j != e:
                        value = jnp.where(lane == j, pltpu.roll(parts[j], ((j - e) * ts) % LANES, 1), value)
                tiles[a * grid_y + e, f] = value * live[e]

    for q in range(count):
        out_tiles[q // slots, q % slots] = tiles[pick[q]] * kept[q]

    sends = []
    for d in range(1, n_tile):
        peer = lax.rem(t + d, n_tile)
        copy = pltpu.make_async_remote_copy(
            src_ref=out_tiles.at[peer], dst_ref=in_tiles.at[t],
            send_sem=all_send.at[d], recv_sem=all_recv.at[d],
            device_id=(peer, c), device_id_type=MESH)
        copy.start()
        sends.append(copy)
    own = pltpu.make_async_copy(out_tiles.at[t], in_tiles.at[t], own_sem)
    own.start()

    def term_step(h, carry):
        base = tiles[h]
        for n, value in enumerate(make_terms(*[base[f] for f in range(5)])):
            terms[n, h] = value
        return carry

    lax.fori_loop(0, count, term_step, 0)

    def gram_step(n, carry):
        mine = terms[n]
        for m in range(TERMS):
            products[n, m * 8:(m + 1) * 8, :] = jnp.sum(mine * terms[m], axis=0)
        return carry

    lax.fori_loop(0, TERMS, gram_step, 0)
    gram_lane = lanes_of((TERMS, LANES))
    part = jnp.zeros((TERMS, LANES), jnp.float32)
    for n in range(TERMS):
        sums = products[n, pl.ds(0, TERMS, stride=8), :]
        for q in range(1, 8):
            sums = sums + products[n, pl.ds(q, TERMS, stride=8), :]
        part = jnp.where(gram_lane == n, jnp.sum(sums, axis=1, keepdims=True), part)
    gram_out[...] = part
    gram_in[t] = part
    first_sums = []
    for d in range(1, n_tile):
        copy = pltpu.make_async_remote_copy(
            src_ref=gram_out, dst_ref=gram_in.at[t],
            send_sem=sum_send.at[d], recv_sem=sum_recv.at[d],
            device_id=(lax.rem(t + d, n_tile), c), device_id_type=MESH)
        copy.start()
        first_sums.append(copy)

    own.wait()
    for copy in sends:
        copy.wait()
    for copy in first_sums:
        copy.wait()
    part = jnp.sum(gram_in[...], axis=0)
    gram_out2[...] = part
    gram_in2[c] = part
    second_sums = []
    for d in range(1, n_col):
        copy = pltpu.make_async_remote_copy(
            src_ref=gram_out2, dst_ref=gram_in2.at[c],
            send_sem=sum2_send.at[d], recv_sem=sum2_recv.at[d],
            device_id=(t, lax.rem(c + d, n_col)), device_id_type=MESH)
        copy.start()
        second_sums.append(copy)

    for copy in second_sums:
        copy.wait()
    gram = jnp.sum(gram_in2[...], axis=0) / (side_rows * side_rows)
    gram_ref[...] = gram[:, :TERMS]


def library_kernel(some, tiles_ref, gram_in_ref, library_ref, gram_ref, block_terms):
    gram_ref[...] = gram_in_ref[...]
    for q in range(some):
        for n, value in enumerate(make_terms(*[tiles_ref[q, f] for f in range(5)])):
            block_terms[q, n * 8:(n + 1) * 8, :] = value
        for s in range(8):
            library_ref[0, 0, q, :, s * LANES:(s + 1) * LANES] = block_terms[q, pl.ds(s, TERMS, stride=8), :]


def per_device(n_tile, n_col, u_velocity, v_velocity, ocean_mask, tile_owner, lower_edge_quarter_turns):
    rows, cols = u_velocity.shape
    grid_x, grid_y = ocean_mask.shape
    count = grid_x * grid_y
    slots = count // n_tile
    planes = cols // LANES + 1
    height = rows + 2 * HALO
    side_rows = rows // 4
    cells = (side_rows // grid_x) ** 2
    vmem = pl.BlockSpec(memory_space=pltpu.VMEM)
    hbm = pl.BlockSpec(memory_space=pltpu.HBM)
    f32 = jnp.float32
    received, gram = pl.pallas_call(
        functools.partial(kernel, n_tile, n_col, grid_x, grid_y),
        out_shape=(
            jax.ShapeDtypeStruct((n_tile, slots, 5, 8, LANES), f32),
            jax.ShapeDtypeStruct((TERMS, TERMS), f32),
        ),
        in_specs=[hbm] * 5,
        out_specs=(vmem, vmem),
        scratch_shapes=[
            pltpu.VMEM((PAIR, cols // LANES, rows, LANES), f32),
            pltpu.SMEM(ocean_mask.shape, jnp.int32),
            pltpu.SMEM(tile_owner.shape, jnp.int32),
            pltpu.SMEM(lower_edge_quarter_turns.shape, jnp.int32),
            pltpu.VMEM((PAIR * planes, height, LANES), f32),
            pltpu.VMEM((planes, height + 16, LANES), f32),
            pltpu.VMEM((planes, height + 16, LANES), f32),
            pltpu.VMEM((planes * LANES, planes * LANES), jnp.bfloat16),
            pltpu.VMEM((planes * LANES, 2 * LANES), jnp.bfloat16),
            pltpu.VMEM((PAIR * planes, height // 4, LANES), f32),
            pltpu.VMEM((PAIR, height // 4, LANES), f32),
            pltpu.VMEM((PAIR, height // 4, LANES), f32),
            pltpu.VMEM((5, side_rows, LANES), f32),
            pltpu.VMEM((count, 5, 8, LANES), f32),
            pltpu.VMEM((TERMS, count, 8, LANES), f32),
            pltpu.VMEM((TERMS, TERMS * 8, LANES), f32),
            pltpu.VMEM((n_tile, slots, 5, 8, LANES), f32),
            pltpu.VMEM((2, PAIR, rows // 8, LANES), f32),
            pltpu.VMEM((2, PAIR, rows // 8, LANES), f32),
            pltpu.VMEM((2, PAIR, HALO, cols), f32),
            pltpu.VMEM((4, PAIR, HALO, LANES), f32),
            pltpu.VMEM((TERMS, LANES), f32),
            pltpu.VMEM((n_tile, TERMS, LANES), f32),
            pltpu.VMEM((TERMS, LANES), f32),
            pltpu.VMEM((n_col, TERMS, LANES), f32),
            pltpu.SMEM((count,), jnp.int32),
            pltpu.SMEM((count,), f32),
            pltpu.SemaphoreType.DMA((PAIR * (cols // LANES) + 3,)),
            pltpu.SemaphoreType.DMA((14,)),
            pltpu.SemaphoreType.DMA((14,)),
            pltpu.SemaphoreType.DMA((n_tile,)),
            pltpu.SemaphoreType.DMA((n_tile,)),
            pltpu.SemaphoreType.DMA((n_tile,)),
            pltpu.SemaphoreType.DMA((n_tile,)),
            pltpu.SemaphoreType.DMA((n_col,)),
            pltpu.SemaphoreType.DMA((n_col,)),
            pltpu.SemaphoreType.DMA,
        ],
        compiler_params=pltpu.CompilerParams(
            collective_id=0, has_side_effects=True, vmem_limit_bytes=60 * 1024 * 1024),
    )(u_velocity, v_velocity, ocean_mask, tile_owner, lower_edge_quarter_turns)
    some = count // 4
    return pl.pallas_call(
        functools.partial(library_kernel, some),
        grid=(4,),
        out_shape=(
            jax.ShapeDtypeStruct((1, 1, count, TERMS, cells), f32),
            jax.ShapeDtypeStruct((TERMS, TERMS), f32),
        ),
        in_specs=[
            pl.BlockSpec((some, 5, 8, LANES), lambda i: (i, 0, 0, 0)),
            pl.BlockSpec((TERMS, TERMS), lambda i: (0, 0)),
        ],
        out_specs=(
            pl.BlockSpec((1, 1, some, TERMS, cells), lambda i: (0, 0, i, 0, 0)),
            pl.BlockSpec((TERMS, TERMS), lambda i: (0, 0)),
        ),
        scratch_shapes=[pltpu.VMEM((some, TERMS * 8, LANES), f32)],
        compiler_params=pltpu.CompilerParams(vmem_limit_bytes=60 * 1024 * 1024),
    )(received.reshape(count, 5, 8, LANES), gram)


def solution(mesh):
    in_specs = (P("tile", "col"), P("tile", "col"), P("tile", "col"), P("tile", "col"), P())
    out_specs = (P("tile", "col", None, None, None), P())
    return jax.shard_map(
        functools.partial(per_device, mesh.shape["tile"], mesh.shape["col"]),
        mesh=mesh, in_specs=in_specs, out_specs=out_specs, check_vma=False,
    )
```
